128 devices in a mesh: ctx: 16 (over y, z), exp: 8 (over x, core).
Axes of the slice: x: 4, y: 4, z: 4, core: 2. Of those that a mesh axis runs over, the one named last changes fastest.
Arguments:
- hidden_in: bfloat16 [8, 3072, 1024], P('exp', 'ctx'), may hold values from -6 to 6
- cotangent: bfloat16 [8, 3072, 1024], P('exp', 'ctx'), may hold values from -6 to 6
- segments: int32 [8, 3072], P('exp'), may hold values from 0 to 3, never falling along the last dimension, each value on 1 to 1536 neighbouring positions
- routes: int32 [8, 3072, 8], P('exp', 'ctx'), may hold values from 0 to 31, all different within a row
- priority: int32 [8, 16, 192], P('exp', 'ctx'), may hold values from 0 to 191, each once within a row
- pair_order: int32 [16], replicated, may hold values from 0 to 15, each once
- attn_gain: bfloat16 [1024], P('exp'), may hold values from 0.099609375 to 1.8984375
- w_query: bfloat16 [1024, 1024], P('exp'), may hold values from -0.1875 to 0.1875
- w_key: bfloat16 [1024, 512], P('exp'), may hold values from -0.1875 to 0.1875
- w_value: bfloat16 [1024, 512], P('exp'), may hold values from -0.1875 to 0.1875
- query_gain: bfloat16 [1024], P('exp'), may hold values from 0.099609375 to 1.8984375
- key_gain: bfloat16 [512], P('exp'), may hold values from 0.099609375 to 1.8984375
- w_output: bfloat16 [1024, 1024], P('exp'), may hold values from -1.75 to 1.75
- ffn_gain: bfloat16 [1024], P('exp'), may hold values from 0.099609375 to 1.8984375
- w_router: bfloat16 [1024, 32], P('exp'), may hold values from -0.109375 to 0.109375
- w_gate: bfloat16 [32, 1024, 512], P('exp', 'ctx'), may hold values from -0.1875 to 0.1875
- w_up: bfloat16 [32, 1024, 512], P('exp', 'ctx'), may hold values from -0.1875 to 0.1875
- w_down: bfloat16 [32, 512, 1024], P('exp', 'ctx'), may hold values from -3 to 3
Outputs:
- layer_out: float32 [8, 3072, 1024], P('exp', 'ctx')
- grad_input: float32 [8, 3072, 1024], P('exp', 'ctx')
- grad_attn_gain: float32 [1024], P('exp')
- grad_query: float32 [1024, 1024], P('exp')
- grad_key: float32 [1024, 512], P('exp')
- grad_value: float32 [1024, 512], P('exp')
- grad_query_gain: float32 [1024], P('exp')
- grad_key_gain: float32 [512], P('exp')
- grad_output: float32 [1024, 1024], P('exp')
- grad_ffn_gain: float32 [1024], P('exp')
- grad_router: float32 [1024, 32], P('exp')
- grad_gate: float32 [32, 1024, 512], P('exp', 'ctx')
- grad_up: float32 [32, 1024, 512], P('exp', 'ctx')
- grad_down: float32 [32, 512, 1024], P('exp', 'ctx')
The draws below stay inside these ranges and needn't reach their ends.
Inputs may be any that keep to these rules, and one draw needn't show every extreme that they name: `routes`: each token names 8 different experts. `priority`: a permutation of the 192 tokens of each device. `pair_order`: a permutation. `segments`: numbers never fall along a sequence and start at 0; every document has 1 to 1536 positions, one exactly 1536.
All inputs are finite; a program needn't handle non-finite values.
Results may differ from the reference program's by a relative error of at most 0.025.
Values may be sent and summed in bfloat16 or wider, within the bound.
A program may use at most 128 MiB of HBM per device.

```python
import math
from functools import partial
import jax
import jax.numpy as jnp
import numpy as np
from jax import lax

D = 1024
HEADS = 16
KV_HEADS = 8
HEAD = 64
FF = 512
TOP = 8
TOK_DEV = 192
EXPERTS = 32
SEQ = 3072
SEQS = 8
CAP = 48
DOCS = 4
N_CTX = 16


def shard_levels(rng, extent, cuts, low, high):
    gain, own = 1.0, jax.random.fold_in(rng, 6)
    for axis_at, blocks in cuts:
        heights = jnp.exp(jax.random.uniform(jax.random.fold_in(own, axis_at), (blocks,), jnp.float32, low / len(cuts), high / len(cuts)))
        gain = gain * jnp.repeat(heights, extent[axis_at] // blocks).reshape([-1 if axis == axis_at else 1 for axis in range(len(extent))])
    return gain


def distinct(key, rows, number_of, top, lift):
    order = jax.random.permutation(jax.random.fold_in(key, 1), number_of)
    pull = order
    for power in range(3):
        pull = pull * pull // number_of
    pull = pull * lift // number_of
    lots = jax.random.randint(jax.random.fold_in(key, 2), (rows, number_of), 0, 4096) + pull
    holders = jax.random.permutation(jax.random.fold_in(key, 3), rows)[jnp.arange(number_of) % rows]
    lots = jnp.where(jnp.arange(rows)[:, None] == holders[None, :], 1 << 14, lots)
    score = lots * number_of + jnp.arange(number_of)
    return lax.top_k(score.astype(jnp.int32), top)[1].astype(jnp.int32)


def length_profile(number_of, total, limit, slope):
    weights = [(1 << 20) // math.isqrt(standing ** slope) + 1 for standing in range(2, number_of + 1)]
    surplus, holding = total - limit - (number_of - 1), [1] * (number_of - 1)
    while surplus > 0:
        free = [i for i in range(number_of - 1) if holding[i] < limit]
        whole, remaining = sum([weights[i] for i in free]), surplus
        for i in free:
            extra = min(limit - holding[i], max(1, remaining * weights[i] // whole), surplus)
            holding[i] = holding[i] + extra
            surplus = surplus - extra
    return np.array([limit] + holding)


def ragged(own_key, amount, total, most, lean):
    if amount == 2:
        one = jax.random.randint(own_key, (), max(1, total - most), min(most, total - 1) + 1)
        return jnp.stack([one, total - one])
    lengths = jnp.asarray(length_profile(amount, total, most, lean), jnp.int32)
    pairs = (amount - 1) // 2
    giver, sink = lengths[1:1 + 2 * pairs:2], lengths[2:2 + 2 * pairs:2]
    room = jnp.minimum(giver - 1, most - sink)
    shifted = jax.random.randint(jax.random.fold_in(own_key, 1), (pairs,), 0, 1 << 20) % (room + 1)
    lengths = lengths.at[1:1 + 2 * pairs:2].set(giver - shifted).at[2:2 + 2 * pairs:2].set(sink + shifted)
    return lengths[jax.random.permutation(jax.random.fold_in(own_key, 2), amount)]


def bell_draw(rng, shape, spread, most, shards=(), held_as=jnp.bfloat16):
    result = jax.random.normal(rng, shape, jnp.float32) * spread
    if len(shards) > 0:
        result = shard_levels(rng, shape, shards, -0.22, 0.18) * result
    return jnp.clip(result, min=-most, max=most).astype(held_as)


def setup_inputs(seed: int = 0) -> dict:
    arg_keys = jax.random.split(jax.random.key(seed), 19)
    hidden_in = bell_draw(arg_keys[0], (SEQS, SEQ, D), 1.0, 6.0, ((0, 8), (1, 16)))
    cotangent = bell_draw(arg_keys[1], (SEQS, SEQ, D), 1.0, 6.0, ((0, 8), (1, 16)))
    segments = jax.vmap(lambda own: jnp.searchsorted(jnp.cumsum(ragged(own, DOCS, SEQ, SEQ // 2, 1)), jnp.arange(SEQ), side="right"))(jax.random.split(arg_keys[2], SEQS)).reshape((SEQS, SEQ)).astype(jnp.int32)
    routes = distinct(arg_keys[3], SEQS * SEQ, EXPERTS, TOP, 2048).reshape((SEQS, SEQ, TOP))
    priority = jax.vmap(lambda own: jax.random.permutation(own, TOK_DEV))(jax.random.split(arg_keys[4], SEQS * N_CTX)).reshape((SEQS, N_CTX, TOK_DEV)).astype(jnp.int32)
    pair_order = jax.random.permutation(arg_keys[5], N_CTX).astype(jnp.int32)
    attn_gain = jnp.clip(1.0 + 0.18 * jax.random.normal(arg_keys[6], (D,), jnp.float32), 0.099609375, 1.8984375).astype(jnp.bfloat16)
    w_query = bell_draw(arg_keys[7], (D, HEADS * HEAD), D ** -0.5, 0.1875, ((0, 8),))
    w_key = bell_draw(arg_keys[8], (D, KV_HEADS * HEAD), D ** -0.5, 0.1875, ((0, 8),))
    w_value = bell_draw(arg_keys[9], (D, KV_HEADS * HEAD), D ** -0.5, 0.1875, ((0, 8),))
    query_gain = jnp.clip(1.0 + 0.18 * jax.random.normal(arg_keys[10], (HEADS * HEAD,), jnp.float32), 0.099609375, 1.8984375).astype(jnp.bfloat16)
    key_gain = jnp.clip(1.0 + 0.18 * jax.random.normal(arg_keys[11], (KV_HEADS * HEAD,), jnp.float32), 0.099609375, 1.8984375).astype(jnp.bfloat16)
    w_output = bell_draw(arg_keys[12], (HEADS * HEAD, D), 0.3, 1.75, ((0, 8),))
    ffn_gain = jnp.clip(1.0 + 0.18 * jax.random.normal(arg_keys[13], (D,), jnp.float32), 0.099609375, 1.8984375).astype(jnp.bfloat16)
    w_router = bell_draw(arg_keys[14], (D, EXPERTS), (0.6 * D ** -0.5), 0.109375, ((0, 8),))
    w_gate = bell_draw(arg_keys[15], (EXPERTS, D, FF), D ** -0.5, 0.1875, ((0, 8), (1, 16)))
    w_up = bell_draw(arg_keys[16], (EXPERTS, D, FF), D ** -0.5, 0.1875, ((0, 8), (1, 16)))
    w_down = bell_draw(arg_keys[17], (EXPERTS, FF, D), (12 * FF ** -0.5), 3.0, ((0, 8), (1, 16)))
    return dict(hidden_in=hidden_in, cotangent=cotangent, segments=segments, routes=routes, priority=priority, pair_order=pair_order, attn_gain=attn_gain, w_query=w_query, w_key=w_key, w_value=w_value, query_gain=query_gain, key_gain=key_gain, w_output=w_output, ffn_gain=ffn_gain, w_router=w_router, w_gate=w_gate, w_up=w_up, w_down=w_down)


@jax.custom_vjp
def low(v):
    return lax.optimization_barrier(v.astype(jnp.bfloat16)).astype(jnp.float32)

@jax.custom_vjp
def low_back(v):
    return v

def low_keep(v):
    return (low(v), None)

def low_pass(kept, grad):
    return (grad,)

def back_keep(v):
    return (v, None)

def back_low(kept, grad):
    return (low(grad),)
low.defvjp(low_keep, low_pass)
low_back.defvjp(back_keep, back_low)
EPS = 1e-06
HIGH = lax.Precision.HIGHEST
MASKED = -1e+30

def normed(values, gain_vec):
    return values * lax.rsqrt(lax.optimization_barrier(jnp.mean(values * values, axis=-1, keepdims=True)) + EPS) * gain_vec

def angles(positions, head_width):
    half_width = head_width // 2
    freqs = 10000.0 ** (-2.0 * jnp.arange(half_width, dtype=jnp.float32) / head_width)
    turned = positions.astype(jnp.float32)[:, None] * freqs[None, :]
    return (jnp.cos(turned), jnp.sin(turned))

def rotate(values, cosine, sine):
    half_width = values.shape[-1] // 2
    first_half = values[..., :half_width]
    second = values[..., half_width:]
    return jnp.concatenate([first_half * cosine - second * sine, second * cosine + first_half * sine], axis=-1)

def stored_positions(pair_order, per_device):
    devices = pair_order.shape[0]
    half_size = per_device // 2
    local_index = jnp.arange(per_device, dtype=jnp.int32)
    in_upper = (local_index >= half_size).astype(jnp.int32)
    offset_in = local_index - in_upper * half_size
    first_block = pair_order.astype(jnp.int32)[:, None]
    chosen_block = first_block + in_upper[None, :] * (2 * devices - 1 - 2 * first_block)
    return (chosen_block * half_size + offset_in[None, :]).reshape(-1)

def assign_slots(routes_block, priority_block, experts, capacity):
    token_count, pick_count = routes_block.shape
    inverse = jnp.zeros((token_count,), jnp.int32).at[priority_block].set(jnp.arange(token_count, dtype=jnp.int32))
    ordered = jnp.take(routes_block, inverse, axis=0)
    flat_ids = ordered.T.reshape(-1)
    one_hot = (flat_ids[:, None] == jnp.arange(experts, dtype=jnp.int32)[None, :]).astype(jnp.int32)
    earlier = jnp.cumsum(one_hot, axis=0) - one_hot
    slot_flat = lax.optimization_barrier(jnp.sum(earlier * one_hot, axis=1))
    slot_index = jnp.take(slot_flat.reshape(pick_count, token_count), priority_block, axis=1).T
    kept_mask = slot_index < capacity
    row_index = routes_block * capacity + jnp.minimum(slot_index, capacity - 1)
    return (row_index, kept_mask)

def slot_tables(row_index, kept_mask, experts, capacity):
    token_count, pick_count = row_index.shape
    target = jnp.where(kept_mask, row_index, experts * capacity).reshape(-1)
    owners = jnp.repeat(jnp.arange(token_count, dtype=jnp.int32), pick_count)
    members = jnp.tile(jnp.arange(pick_count, dtype=jnp.int32), token_count)
    slot_token = jnp.zeros((experts * capacity,), jnp.int32).at[target].set(owners, mode='drop')
    slot_member = jnp.zeros((experts * capacity,), jnp.int32).at[target].set(members, mode='drop')
    slot_live = jnp.zeros((experts * capacity,), jnp.float32).at[target].set(1.0, mode='drop')
    return (slot_token, slot_member, slot_live)

def forward(positions, doc_ids, slot_token, slot_member, slot_live, routes, hidden_in, attn_gain, w_query, w_key, w_value, query_gain, key_gain, w_output, ffn_gain, w_router, w_gate, w_up, w_down):
    seq_count, length, model_width = hidden_in.shape
    group_size = HEADS // KV_HEADS
    score_scale = HEAD ** (-0.5)
    normed_in = low(normed(hidden_in, attn_gain))
    query_proj = low_back(jnp.einsum('std,de->ste', normed_in, w_query, precision=HIGH))
    key_proj = low_back(jnp.einsum('std,de->ste', normed_in, w_key, precision=HIGH))
    value_all = low(low_back(jnp.einsum('std,de->ste', normed_in, w_value, precision=HIGH)))
    cosine, sine = angles(positions, HEAD)
    cosine = cosine[:, None, :]
    sine = sine[:, None, :]
    query_rot = low(rotate(normed(query_proj, query_gain).reshape(seq_count, length, HEADS, HEAD), cosine, sine))
    key_rot = low(rotate(normed(key_proj, key_gain).reshape(seq_count, length, KV_HEADS, HEAD), cosine, sine))

    def attend_item(packed):
        query_item, key_item, value_item, doc_item = packed
        scores = low_back(jnp.einsum('qgh,kh->gqk', query_item, key_item, precision=HIGH) * score_scale)
        allowed = (doc_item[:, None] == doc_item[None, :]) & (positions[None, :] <= positions[:, None])
        scores = jnp.where(allowed[None], scores, MASKED)
        row_peak = lax.optimization_barrier(jnp.max(scores, axis=-1, keepdims=True))
        weights = jnp.exp(scores - row_peak)
        probs_low = low(weights / lax.optimization_barrier(jnp.sum(weights, axis=-1, keepdims=True)))
        return jnp.einsum('gqk,kh->qgh', probs_low, value_item, precision=HIGH)
    query_items = query_rot.reshape(seq_count, length, KV_HEADS, group_size, HEAD).transpose(0, 2, 1, 3, 4).reshape(seq_count * KV_HEADS, length, group_size, HEAD)
    key_items = key_rot.transpose(0, 2, 1, 3).reshape(seq_count * KV_HEADS, length, HEAD)
    value_items = value_all.reshape(seq_count, length, KV_HEADS, HEAD).transpose(0, 2, 1, 3).reshape(seq_count * KV_HEADS, length, HEAD)
    doc_items = jnp.repeat(doc_ids, KV_HEADS, axis=0)
    mixed = lax.map(jax.checkpoint(attend_item), (query_items, key_items, value_items, doc_items))
    mixed = mixed.reshape(seq_count, KV_HEADS, length, group_size, HEAD).transpose(0, 2, 1, 3, 4).reshape(seq_count, length, HEADS * HEAD)
    attended = low(low_back(mixed))
    after_attn = hidden_in + low_back(jnp.einsum('ste,ed->std', attended, w_output, precision=HIGH))
    normed_mid = low(normed(after_attn, ffn_gain))
    logits = jnp.einsum('std,de->ste', normed_mid, w_router, precision=HIGH)
    gates = jnp.take_along_axis(jax.nn.softmax(logits, axis=-1), routes, axis=-1)
    blocks = seq_count * length // TOK_DEV

    def expert_block(packed):
        normed_block, gate_block, token_ids, member_ids, live_ids = packed
        dispatched = low_back(jnp.take(normed_block, token_ids, axis=0) * live_ids[:, None]).reshape(EXPERTS, CAP, model_width)
        gate_act = low_back(jnp.einsum('ecd,edf->ecf', dispatched, w_gate, precision=HIGH))
        up_act = low_back(jnp.einsum('ecd,edf->ecf', dispatched, w_up, precision=HIGH))
        inner_low = low(jax.nn.silu(gate_act) * up_act)
        returned = low(low_back(jnp.einsum('ecf,efd->ecd', inner_low, w_down, precision=HIGH))).reshape(EXPERTS * CAP, model_width)
        slot_weight = gate_block[token_ids, member_ids] * live_ids
        return jnp.zeros_like(normed_block).at[token_ids].add(slot_weight[:, None] * returned)
    mixture = lax.map(jax.checkpoint(expert_block), (normed_mid.reshape(blocks, TOK_DEV, model_width), gates.reshape(blocks, TOK_DEV, TOP), slot_token, slot_member, slot_live))
    return after_attn + mixture.reshape(seq_count, length, model_width)

def reference(hidden_in, cotangent, segments, routes, priority, pair_order, attn_gain, w_query, w_key, w_value, query_gain, key_gain, w_output, ffn_gain, w_router, w_gate, w_up, w_down):
    positions = stored_positions(pair_order, TOK_DEV)
    doc_ids = jnp.take(segments, positions, axis=1)
    blocks = SEQS * N_CTX
    row_index, kept_mask = jax.vmap(partial(assign_slots, experts=EXPERTS, capacity=CAP))(routes.reshape(blocks, TOK_DEV, TOP), priority.reshape(blocks, TOK_DEV))
    slot_token, slot_member, slot_live = jax.vmap(partial(slot_tables, experts=EXPERTS, capacity=CAP))(row_index, kept_mask)
    floats = [array_in.astype(jnp.float32) for array_in in (hidden_in, attn_gain, w_query, w_key, w_value, query_gain, key_gain, w_output, ffn_gain, w_router, w_gate, w_up, w_down)]
    layer_out, pullback = jax.vjp(partial(forward, positions, doc_ids, slot_token, slot_member, slot_live, routes), *floats)
    gradients = pullback(cotangent.astype(jnp.float32))
    return (layer_out, gradients[0], gradients[1], gradients[2], gradients[3], gradients[4], gradients[5], gradients[6], gradients[7], gradients[8], gradients[9], gradients[10], gradients[11], gradients[12])
```

```python
import functools

import jax
import jax.numpy as jnp
from jax import lax
from jax.experimental import pallas as pl
from jax.experimental.pallas import tpu as pltpu
from jax.sharding import PartitionSpec as P

MESH = pl.DeviceIdType.MESH
BF = jnp.bfloat16
F32 = jnp.float32
HEADS = 16
KV_HEADS = 8
HEAD = 64
TOP = 8
EXP_DEV = 4
EXPERTS = 32
TOK = 192
HALF = 96
D = 1024
FF = 512
CAP = 48
SEQ = 3072
TILE = 256
WIDE = D + 128
PACK = 3328
EPS = 1e-06
HIGH = lax.Precision.HIGHEST
MASKED = -1e30
VMEM_BYTES = 60 * 1024 * 1024


class Place:
    def __init__(self):
        self.c = lax.axis_index("ctx")
        self.e = lax.axis_index("exp")
        self.x, self.k = self.e // 2, self.e % 2
        self.y, self.z = self.c // 4, self.c % 4

    def exp_at(self, shift):
        return ((self.x + shift) % 4) * 2 + self.k

    def along_x(self, shift):
        return (self.c, self.exp_at(shift))

    def sibling(self):
        return (self.c, self.x * 2 + 1 - self.k)

    def ctx_at(self, half, first, second):
        if half == 0:
            return ((self.y + second) % 4) * 4 + (self.z + first) % 4
        return ((self.y + first) % 4) * 4 + (self.z + second) % 4

    def along_first(self, half, shift):
        return (self.ctx_at(half, shift, 0), self.e)

    def along_second(self, half, shift):
        return (self.ctx_at(half, 0, shift), self.e)

    def ctx_ahead(self, shift):
        return (self.c + shift) % 16


class Mail:
    def __init__(self, send_sems, recv_sems, place):
        self.send_sems, self.recv_sems, self.place = send_sems, recv_sems, place
        self.used, self.sent = 0, []

    def slots(self, number):
        first = self.used
        self.used += number
        return list(range(first, first + number))

    def send(self, slot, src, dst, device):
        copy = pltpu.make_async_remote_copy(
            src_ref=src,
            dst_ref=dst,
            send_sem=self.send_sems.at[slot],
            recv_sem=self.recv_sems.at[slot],
            device_id=device,
            device_id_type=MESH,
        )
        copy.start()
        self.sent.append(copy)

    def wait(self, slot, region):
        pltpu.make_async_remote_copy(
            src_ref=region,
            dst_ref=region,
            send_sem=self.send_sems.at[slot],
            recv_sem=self.recv_sems.at[slot],
            device_id=self.place.sibling(),
            device_id_type=MESH,
        ).wait_recv()

    def finish(self):
        for copy in self.sent:
            copy.wait_send()
        self.sent = []


def meet(devices):
    barrier = pltpu.get_barrier_semaphore()
    for device in devices:
        pl.semaphore_signal(barrier, inc=1, device_id=device, device_id_type=MESH)
    pl.semaphore_wait(barrier, len(devices))


def ring_x_peers(place):
    return [place.along_x(1), place.along_x(3), place.sibling()]


def ring_yz_peers(place):
    return [
        place.along_first(0, 1),
        place.along_first(0, 3),
        place.along_first(1, 1),
        place.along_first(1, 3),
    ]


def ctx_peers(place):
    return [(place.ctx_ahead(shift), place.e) for shift in range(1, 16)]


def interleave(routines):
    routines = list(routines)
    while routines:
        for routine in list(routines):
            try:
                next(routine)
            except StopIteration:
                routines.remove(routine)


def gather_x(place, mail, out, rows):
    (to_right, to_left, to_sib, far0, far1, sib_l, sib_r, sib_f0, sib_f1) = mail.slots(9)
    half = rows // 2

    def shard(shift, core_same=True):
        exp = place.exp_at(shift) if core_same else place.exp_at(shift) + 1 - 2 * place.k
        return out.at[pl.ds(pl.multiple_of(exp * rows, 16), rows)]

    def part(shift, which, core_same=True):
        exp = place.exp_at(shift) if core_same else place.exp_at(shift) + 1 - 2 * place.k
        return out.at[pl.ds(pl.multiple_of(exp * rows + which * half, 16), half)]

    right, left, sib = place.along_x(1), place.along_x(3), place.sibling()
    mail.send(to_right, shard(0), shard(0), right)
    mail.send(to_left, shard(0), shard(0), left)
    mail.send(to_sib, shard(0), shard(0), sib)
    yield
    mail.wait(to_right, shard(3))
    mail.send(far0, part(3, 0), part(3, 0), right)
    mail.send(sib_l, shard(3), shard(3), sib)
    mail.wait(to_left, shard(1))
    mail.send(far1, part(1, 1), part(1, 1), left)
    mail.send(sib_r, shard(1), shard(1), sib)
    yield
    mail.wait(far0, part(2, 0))
    mail.send(sib_f0, part(2, 0), part(2, 0), sib)
    mail.wait(far1, part(2, 1))
    mail.send(sib_f1, part(2, 1), part(2, 1), sib)
    yield
    mail.wait(to_sib, shard(0, False))
    mail.wait(sib_l, shard(3, False))
    mail.wait(sib_r, shard(1, False))
    mail.wait(sib_f0, part(2, 0, False))
    mail.wait(sib_f1, part(2, 1, False))


def gather_yz(place, mail, out, half):
    first, second = (functools.partial(f, half) for f in (place.along_first, place.along_second))

    def piece(a, b):
        return out.at[pl.ds(2 * half, 2), place.ctx_at(half, a, b)]

    def quarter(a, b, which):
        return out.at[2 * half + which, place.ctx_at(half, a, b)]

    f_r, f_l, f_far0, f_far1 = mail.slots(4)
    mail.send(f_r, piece(0, 0), piece(0, 0), first(1))
    mail.send(f_l, piece(0, 0), piece(0, 0), first(3))
    s_slots = {a: mail.slots(2) for a in (0, 1, 3)}
    s_far = {a: mail.slots(2) for a in (0, 1, 2, 3)}
    s_quarters = mail.slots(4)
    mail.send(s_slots[0][0], piece(0, 0), piece(0, 0), second(1))
    mail.send(s_slots[0][1], piece(0, 0), piece(0, 0), second(3))
    yield
    mail.wait(f_r, piece(3, 0))
    mail.send(f_far0, quarter(3, 0, 0), quarter(3, 0, 0), first(1))
    mail.wait(f_l, piece(1, 0))
    mail.send(f_far1, quarter(1, 0, 1), quarter(1, 0, 1), first(3))
    for a in (3, 1):
        mail.send(s_slots[a][0], piece(a, 0), piece(a, 0), second(1))
        mail.send(s_slots[a][1], piece(a, 0), piece(a, 0), second(3))
    yield
    mail.wait(s_slots[0][0], piece(0, 3))
    mail.send(s_far[0][0], quarter(0, 3, 0), quarter(0, 3, 0), second(1))
    mail.wait(s_slots[0][1], piece(0, 1))
    mail.send(s_far[0][1], quarter(0, 1, 1), quarter(0, 1, 1), second(3))
    mail.wait(f_far0, quarter(2, 0, 0))
    mail.send(s_quarters[0], quarter(2, 0, 0), quarter(2, 0, 0), second(1))
    mail.send(s_quarters[1], quarter(2, 0, 0), quarter(2, 0, 0), second(3))
    mail.wait(f_far1, quarter(2, 0, 1))
    mail.send(s_quarters[2], quarter(2, 0, 1), quarter(2, 0, 1), second(1))
    mail.send(s_quarters[3], quarter(2, 0, 1), quarter(2, 0, 1), second(3))
    yield
    for a in (3, 1):
        mail.wait(s_slots[a][0], piece(a, 3))
        mail.send(s_far[a][0], quarter(a, 3, 0), quarter(a, 3, 0), second(1))
        mail.wait(s_slots[a][1], piece(a, 1))
        mail.send(s_far[a][1], quarter(a, 1, 1), quarter(a, 1, 1), second(3))
    yield
    mail.wait(s_quarters[0], quarter(2, 3, 0))
    mail.send(s_far[2][0], quarter(2, 3, 0), quarter(2, 3, 0), second(1))
    mail.wait(s_quarters[3], quarter(2, 1, 1))
    mail.send(s_far[2][1], quarter(2, 1, 1), quarter(2, 1, 1), second(3))
    mail.wait(s_quarters[1], quarter(2, 1, 0))
    mail.wait(s_quarters[2], quarter(2, 3, 1))
    yield
    for a in (0, 1, 2, 3):
        mail.wait(s_far[a][0], quarter(a, 2, 0))
        mail.wait(s_far[a][1], quarter(a, 2, 1))


GATHER_YZ_COPIES = 2 * 22


def add_rows(out, terms, rows, step=16):
    def body(i, _):
        at = pl.ds(pl.multiple_of(i * step, step), step)
        total = terms[0][at].astype(F32)
        for term in terms[1:]:
            total = total + term[at].astype(F32)
        out[at] = total.astype(out.dtype)
        return 0

    lax.fori_loop(0, rows // step, body, 0)


def scatter_x(place, mail, grads, out, sib_buf, sums, near, far, rows):
    half = rows // 2
    s_sib = mail.slots(4)
    far0, far1, r_free, r_dep, l_free, l_dep = mail.slots(6)
    right, left, sib = place.along_x(1), place.along_x(3), place.sibling()
    order = (2, 1, 3, 0)
    for at, shift in enumerate(order):
        theirs = place.exp_at(shift) + 1 - 2 * place.k
        mail.send(s_sib[at], grads.at[theirs], sib_buf.at[at], sib)
    yield

    def mine(shift, which):
        return grads.at[place.exp_at(shift), pl.ds(which * half, half)]

    def from_sib(at, which):
        return sib_buf.at[at, pl.ds(which * half, half)]

    mail.wait(s_sib[0], sib_buf.at[0])
    add_rows(sums.at[0, 0], [mine(2, 0), from_sib(0, 0)], half)
    mail.send(far0, sums.at[0, 0], far.at[0], right)
    add_rows(sums.at[0, 1], [mine(2, 1), from_sib(0, 1)], half)
    mail.send(far1, sums.at[0, 1], far.at[1], left)
    yield
    mail.wait(s_sib[1], sib_buf.at[1])
    add_rows(sums.at[1, 1], [mine(1, 1), from_sib(1, 1)], half)
    mail.send(r_free, sums.at[1, 1], near.at[0, 1], right)
    mail.wait(s_sib[2], sib_buf.at[2])
    add_rows(sums.at[2, 0], [mine(3, 0), from_sib(2, 0)], half)
    mail.send(l_free, sums.at[2, 0], near.at[1, 0], left)
    yield
    mail.wait(far0, far.at[0])
    add_rows(sums.at[1, 0], [mine(1, 0), from_sib(1, 0), far.at[0]], half)
    mail.send(r_dep, sums.at[1, 0], near.at[0, 0], right)
    mail.wait(far1, far.at[1])
    add_rows(sums.at[2, 1], [mine(3, 1), from_sib(2, 1), far.at[1]], half)
    mail.send(l_dep, sums.at[2, 1], near.at[1, 1], left)
    yield
    mail.wait(s_sib[3], sib_buf.at[3])
    mail.wait(r_free, near.at[0, 1])
    mail.wait(l_free, near.at[1, 0])
    mail.wait(r_dep, near.at[0, 0])
    mail.wait(l_dep, near.at[1, 1])
    for which in (0, 1):
        add_rows(
            out.at[pl.ds(which * half, half)],
            [mine(0, which), from_sib(3, which), near.at[0, which], near.at[1, which]],
            half,
        )


SCATTER_X_COPIES = 10


def scatter_x_scratch(rows, columns):
    half = rows // 2
    return [
        pltpu.VMEM((4, rows, columns), BF),
        pltpu.VMEM((3, 2, half, columns), BF),
        pltpu.VMEM((2, 2, half, columns), BF),
        pltpu.VMEM((2, half, columns), BF),
    ]


def scatter_yz(place, mail, grads, out, half, far, near, sums, mid, far2, near2, sums2):
    first, second = (functools.partial(f, half) for f in (place.along_first, place.along_second))
    rows = grads.shape[2]

    def quarter(a, b, which):
        return grads.at[2 * half + which, place.ctx_at(half, a, b)]

    order = (2, 1, 3, 0)
    sl_far = {a: mail.slots(2) for a in order}
    sl_free = {a: mail.slots(2) for a in order}
    sl_dep = {a: mail.slots(2) for a in order}
    for at, a in enumerate(order):
        mail.send(sl_far[a][0], quarter(a, 2, 0), far.at[half, 0, at], second(1))
        mail.send(sl_far[a][1], quarter(a, 2, 1), far.at[half, 1, at], second(3))
        mail.send(sl_free[a][0], quarter(a, 1, 1), near.at[half, 0, 1, at], second(1))
        mail.send(sl_free[a][1], quarter(a, 3, 0), near.at[half, 1, 0, at], second(3))
    yield
    for at, a in enumerate(order):
        mail.wait(sl_far[a][0], far.at[half, 0, at])
        add_rows(sums.at[half, 0, at], [quarter(a, 1, 0), far.at[half, 0, at]], rows)
        mail.send(sl_dep[a][0], sums.at[half, 0, at], near.at[half, 0, 0, at], second(1))
        mail.wait(sl_far[a][1], far.at[half, 1, at])
        add_rows(sums.at[half, 1, at], [quarter(a, 3, 1), far.at[half, 1, at]], rows)
        mail.send(sl_dep[a][1], sums.at[half, 1, at], near.at[half, 1, 1, at], second(3))
        yield
    m_far, m_free, m_dep = mail.slots(2), mail.slots(2), mail.slots(2)
    for at, a in enumerate(order):
        mail.wait(sl_free[a][0], near.at[half, 0, 1, at])
        mail.wait(sl_free[a][1], near.at[half, 1, 0, at])
        mail.wait(sl_dep[a][0], near.at[half, 0, 0, at])
        mail.wait(sl_dep[a][1], near.at[half, 1, 1, at])
        for which in (0, 1):
            add_rows(
                mid.at[half, which, at],
                [quarter(a, 0, which), near.at[half, 0, which, at], near.at[half, 1, which, at]],
                rows,
            )
        if a == 2:
            mail.send(m_far[0], mid.at[half, 0, at], far2.at[half, 0], first(1))
            mail.send(m_far[1], mid.at[half, 1, at], far2.at[half, 1], first(3))
        if a == 1:
            mail.send(m_free[0], mid.at[half, 1, at], near2.at[half, 0, 1], first(1))
        if a == 3:
            mail.send(m_free[1], mid.at[half, 0, at], near2.at[half, 1, 0], first(3))
        yield
    mail.wait(m_far[0], far2.at[half, 0])
    add_rows(sums2.at[half, 0], [mid.at[half, 0, 1], far2.at[half, 0]], rows)
    mail.send(m_dep[0], sums2.at[half, 0], near2.at[half, 0, 0], first(1))
    mail.wait(m_far[1], far2.at[half, 1])
    add_rows(sums2.at[half, 1], [mid.at[half, 1, 2], far2.at[half, 1]], rows)
    mail.send(m_dep[1], sums2.at[half, 1], near2.at[half, 1, 1], first(3))
    yield
    mail.wait(m_free[0], near2.at[half, 0, 1])
    mail.wait(m_free[1], near2.at[half, 1, 0])
    mail.wait(m_dep[0], near2.at[half, 0, 0])
    mail.wait(m_dep[1], near2.at[half, 1, 1])
    for which in (0, 1):
        add_rows(
            out.at[2 * half + which],
            [mid.at[half, which, 3], near2.at[half, 0, which], near2.at[half, 1, which]],
            rows,
        )


SCATTER_YZ_COPIES = 2 * 30


def scatter_yz_scratch(rows, columns):
    one = (rows, columns)
    return [
        pltpu.VMEM((2, 2, 4) + one, BF),
        pltpu.VMEM((2, 2, 2, 4) + one, BF),
        pltpu.VMEM((2, 2, 4) + one, BF),
        pltpu.VMEM((2, 2, 4) + one, BF),
        pltpu.VMEM((2, 2) + one, BF),
        pltpu.VMEM((2, 2, 2) + one, BF),
        pltpu.VMEM((2, 2) + one, BF),
    ]


SUM_ROWS = 16
SUM_COLUMNS = PACK // 2


def sum_ctx(place, mail, mine, out, slots):
    up, down = mail.slots(15), mail.slots(15)

    def piece(ref, c):
        return ref.at[
            pl.ds(pl.multiple_of((c // 2) * SUM_ROWS, SUM_ROWS), SUM_ROWS),
            pl.ds(pl.multiple_of((c % 2) * SUM_COLUMNS, 128), SUM_COLUMNS),
        ]

    for shift in range(1, 16):
        c = place.ctx_ahead(shift)
        mail.send(up[shift - 1], piece(mine, c), slots.at[shift], (c, place.e))
    yield
    for shift in range(1, 16):
        mail.wait(up[shift - 1], slots.at[shift])
    total = piece(mine, place.c)[...].astype(F32)
    for shift in range(1, 16):
        total = total + slots[shift].astype(F32)
    own = piece(out, place.c)
    own[...] = total.astype(BF)
    for shift in range(1, 16):
        c = place.ctx_ahead(shift)
        mail.send(down[shift - 1], own, own, (c, place.e))
    yield
    for shift in range(1, 16):
        mail.wait(down[shift - 1], piece(out, place.ctx_ahead(16 - shift)))


def any_spec():
    return pl.BlockSpec(memory_space=pl.ANY)


def vmem_spec():
    return pl.BlockSpec(memory_space=pltpu.VMEM)


def sends(body, number, outs, args, in_specs, out_specs, scratch, collective_id):
    return pl.pallas_call(
        body,
        out_shape=outs,
        in_specs=in_specs,
        out_specs=out_specs,
        scratch_shapes=list(scratch)
        + [pltpu.SemaphoreType.DMA((number,)), pltpu.SemaphoreType.DMA((number,))],
        compiler_params=pltpu.CompilerParams(
            collective_id=collective_id, has_side_effects=True, vmem_limit_bytes=VMEM_BYTES
        ),
    )(*args)


def first_body(
    w_query, w_key, w_value, w_output, misc, cot, slots, w_gate, w_up, w_down,
    dense, cots, experts, local_sems, send_sems, recv_sems,
):
    place = Place()
    mail = Mail(send_sems, recv_sems, place)
    row = pl.ds(pl.multiple_of(place.e * 128, 128), 128)
    tok = pl.ds(pl.multiple_of(place.e * TOK, TOK), TOK)
    pairs = [
        (w_gate, experts.at[:, place.c, pl.ds(0, 64), pl.ds(0, FF)]),
        (w_up, experts.at[:, place.c, pl.ds(0, 64), pl.ds(FF, FF)]),
        (w_down, experts.at[:, place.c, pl.ds(64, 32), :]),
        (w_query, dense.at[row, pl.ds(0, 1024)]),
        (w_key, dense.at[row, pl.ds(1024, 512)]),
        (w_value, dense.at[row, pl.ds(1536, 512)]),
        (w_output, dense.at[row, pl.ds(2048, 1024)]),
        (misc, dense.at[row, pl.ds(3072, 256)]),
        (cot, cots.at[tok, pl.ds(0, D)]),
        (slots, cots.at[tok, pl.ds(D, 128)]),
    ]
    copies = [
        pltpu.make_async_copy(src, dst, local_sems.at[i]) for i, (src, dst) in enumerate(pairs)
    ]
    for copy in copies:
        copy.start()
    for copy in copies:
        copy.wait()
    meet(ring_x_peers(place) + ring_yz_peers(place))
    interleave(
        [
            gather_yz(place, mail, experts, 0),
            gather_yz(place, mail, experts, 1),
            gather_x(place, mail, dense, 128),
            gather_x(place, mail, cots, TOK),
        ]
    )
    mail.finish()


def first_gather(*args):
    number = GATHER_YZ_COPIES + 18
    return sends(
        first_body,
        number,
        [
            jax.ShapeDtypeStruct((1024, PACK), BF),
            jax.ShapeDtypeStruct((8 * TOK, WIDE), BF),
            jax.ShapeDtypeStruct((4, 16, 96, 1024), BF),
        ],
        args,
        [any_spec()] * 10,
        [any_spec()] * 3,
        [pltpu.SemaphoreType.DMA((10,))],
        1,
    )


def exchange_body(src, dst, local_sem, send_sems, recv_sems):
    place = Place()
    mail = Mail(send_sems, recv_sems, place)
    own = pltpu.make_async_copy(src.at[place.c], dst.at[place.c], local_sem)
    own.start()
    meet(ctx_peers(place))
    slots = mail.slots(15)
    for shift in range(1, 16):
        c = place.ctx_ahead(shift)
        mail.send(slots[shift - 1], src.at[c], dst.at[place.c], (c, place.e))
    for shift in range(1, 16):
        mail.wait(slots[shift - 1], dst.at[place.ctx_ahead(16 - shift)])
    own.wait()
    mail.finish()


def exchange(blocks, collective_id):
    return sends(
        exchange_body,
        15,
        jax.ShapeDtypeStruct(blocks.shape, blocks.dtype),
        (blocks,),
        [any_spec()],
        any_spec(),
        [pltpu.SemaphoreType.DMA],
        collective_id,
    )


def tokens_body(rows, out, local_sem, send_sems, recv_sems):
    place = Place()
    mail = Mail(send_sems, recv_sems, place)
    own = pltpu.make_async_copy(rows, out.at[pl.ds(pl.multiple_of(place.e * TOK, TOK), TOK)], local_sem)
    own.start()
    own.wait()
    meet(ring_x_peers(place))
    interleave([gather_x(place, mail, out, TOK)])
    mail.finish()


def tokens_gather(rows):
    return sends(
        tokens_body,
        9,
        jax.ShapeDtypeStruct((8 * TOK, WIDE), BF),
        (rows,),
        [any_spec()],
        any_spec(),
        [pltpu.SemaphoreType.DMA],
        2,
    )


def combine_body(mids, outs, mid, out, *rest):
    send_sems, recv_sems = rest[-2:]
    place = Place()
    mail = Mail(send_sems, recv_sems, place)
    meet(ring_x_peers(place))
    interleave(
        [
            scatter_x(place, mail, mids, mid, *rest[0:4], TOK),
            scatter_x(place, mail, outs, out, *rest[4:8], TOK),
        ]
    )
    mail.finish()


def combine(mids, outs):
    return sends(
        combine_body,
        2 * SCATTER_X_COPIES,
        [
            jax.ShapeDtypeStruct((TOK, WIDE), F32),
            jax.ShapeDtypeStruct((TOK, D), F32),
        ],
        (mids, outs),
        [vmem_spec()] * 2,
        [vmem_spec()] * 2,
        scatter_x_scratch(TOK, WIDE) + scatter_x_scratch(TOK, D),
        3,
    )


def last_body(experts, dense, experts_out, dense_out, *rest):
    yz, x = rest[0:7], rest[7:11]
    mine, slots, send_sems, recv_sems = rest[11:]
    place = Place()
    mail = Mail(send_sems, recv_sems, place)
    meet(ring_x_peers(place) + ctx_peers(place))

    def dense_sum():
        yield from scatter_x(place, mail, dense, mine, *x, 128)
        yield from sum_ctx(place, mail, mine, dense_out, slots)

    interleave(
        [
            dense_sum(),
            scatter_yz(place, mail, experts, experts_out, 0, *yz),
            scatter_yz(place, mail, experts, experts_out, 1, *yz),
        ]
    )
    mail.finish()


def last_sum(experts, dense):
    return sends(
        last_body,
        SCATTER_YZ_COPIES + SCATTER_X_COPIES + 30,
        [
            jax.ShapeDtypeStruct((4, 96, 1024), F32),
            jax.ShapeDtypeStruct((128, PACK), BF),
        ],
        (experts, dense),
        [vmem_spec()] * 2,
        [vmem_spec()] * 2,
        scatter_yz_scratch(96, 1024)
        + scatter_x_scratch(128, PACK)
        + [pltpu.VMEM((128, PACK), BF), pltpu.VMEM((16, SUM_ROWS, SUM_COLUMNS), BF)],
        4,
    )


def dot_tt(a, b, dims):
    return lax.dot_general(a, b, (dims, ((), ())), preferred_element_type=F32)


def open_blocks(order, src, which, dst, scale=None):
    def body(c, _):
        block = src[c, which]
        low, high = block[:, 0:HEAD], block[:, HEAD : 2 * HEAD]
        if scale is not None:
            low, high = low * scale, high * scale
        spot = order[c]
        dst[pl.ds(pl.multiple_of(spot * HALF, 16), HALF), :] = low
        dst[pl.ds(pl.multiple_of((31 - spot) * HALF, 16), HALF), :] = high
        return 0

    lax.fori_loop(0, 16, body, 0)


def close_blocks(order, src, dst, which):
    def body(c, _):
        spot = order[c]
        low = src[pl.ds(pl.multiple_of(spot * HALF, 16), HALF), :]
        high = src[pl.ds(pl.multiple_of((31 - spot) * HALF, 16), HALF), :]
        dst[c, which] = jnp.concatenate([low, high], axis=1).astype(dst.dtype)
        return 0

    lax.fori_loop(0, 16, body, 0)


def tile_mask(bounds, i, j):
    query_at = lax.broadcasted_iota(jnp.int32, (1, TILE), 1) + i * TILE
    key_at = lax.broadcasted_iota(jnp.int32, (TILE, TILE), 0) + j * TILE
    start = jnp.zeros((1, TILE), jnp.int32)
    for d in range(3):
        start = jnp.where(query_at >= bounds[d], bounds[d], start)
    return (key_at >= start) & (key_at <= query_at)


def attend_body(order, bounds, first_tile, qkv, attended, kept, qs, ks, vs, vt, outs):
    open_blocks(order, qkv, 0, qs, 0.125)
    open_blocks(order, qkv, 1, ks)
    open_blocks(order, qkv, 2, vs)

    def turn(i, _):
        at = pl.ds(pl.multiple_of(i * TILE, TILE), TILE)
        vt[:, at] = vs[at, :].astype(F32).T.astype(BF)
        return 0

    lax.fori_loop(0, SEQ // TILE, turn, 0)

    def query_tile(i, _):
        at = pl.ds(pl.multiple_of(i * TILE, TILE), TILE)
        query = qs[at, :]

        def key_tile(j, state):
            peak, total, acc = state
            here = pl.ds(pl.multiple_of(j * TILE, TILE), TILE)
            scores = dot_tt(ks[here, :], query, ((1,), (1,)))
            scores = jnp.where(tile_mask(bounds, i, j), scores, MASKED)
            new_peak = jnp.maximum(peak, jnp.max(scores, axis=0, keepdims=True))
            weights = jnp.exp(scores - new_peak)
            keep = jnp.exp(peak - new_peak)
            total = total * keep + jnp.sum(weights, axis=0, keepdims=True)
            acc = acc * keep + dot_tt(vt[:, here], weights.astype(BF), ((1,), (0,)))
            return new_peak, total, acc

        peak, total, acc = lax.fori_loop(
            first_tile[i],
            i + 1,
            key_tile,
            (
                jnp.full((1, TILE), MASKED, F32),
                jnp.zeros((1, TILE), F32),
                jnp.zeros((HEAD, TILE), F32),
            ),
        )
        mixed = acc / total
        kept[0:HEAD, at] = mixed
        kept[HEAD : HEAD + 8, at] = jnp.broadcast_to(peak + jnp.log(total), (8, TILE))
        outs[at, :] = mixed.T
        return 0

    lax.fori_loop(0, SEQ // TILE, query_tile, 0)
    close_blocks(order, outs, attended, 0)


def smem_spec():
    return pl.BlockSpec(memory_space=pltpu.SMEM)


def attend(order, bounds, first_tile, qkv):
    return pl.pallas_call(
        attend_body,
        out_shape=[
            jax.ShapeDtypeStruct((16, 1, HALF, 2 * HEAD), BF),
            jax.ShapeDtypeStruct((HEAD + 8, SEQ), F32),
        ],
        in_specs=[smem_spec()] * 3 + [vmem_spec()],
        out_specs=[vmem_spec()] * 2,
        scratch_shapes=[pltpu.VMEM((SEQ, HEAD), BF)] * 3
        + [pltpu.VMEM((HEAD, SEQ), BF), pltpu.VMEM((SEQ, HEAD), F32)],
        compiler_params=pltpu.CompilerParams(vmem_limit_bytes=VMEM_BYTES),
    )(order, bounds, first_tile, qkv)


def attend_back_body(
    order, bounds, first_tile, qkv, grad_in, kept, grads,
    qs, ks, vs, gs, kt, dq, dk, dv,
):
    open_blocks(order, qkv, 0, qs, 0.125)
    open_blocks(order, qkv, 1, ks)
    open_blocks(order, qkv, 2, vs)
    open_blocks(order, grad_in, 0, gs)
    dk[...] = jnp.zeros_like(dk)
    dv[...] = jnp.zeros_like(dv)

    def turn(i, _):
        at = pl.ds(pl.multiple_of(i * TILE, TILE), TILE)
        kt[:, at] = ks[at, :].astype(F32).T.astype(BF)
        return 0

    lax.fori_loop(0, SEQ // TILE, turn, 0)

    def query_tile(i, _):
        at = pl.ds(pl.multiple_of(i * TILE, TILE), TILE)
        query = qs[at, :]
        grad = gs[at, :]
        mixed = kept[0:HEAD, at]
        lse = kept[HEAD : HEAD + 1, at]
        delta = jnp.sum(mixed * grad.astype(F32).T, axis=0, keepdims=True)

        def key_tile(j, acc):
            here = pl.ds(pl.multiple_of(j * TILE, TILE), TILE)
            scores = dot_tt(ks[here, :], query, ((1,), (1,)))
            scores = jnp.where(tile_mask(bounds, i, j), scores, MASKED)
            probs = jnp.exp(scores - lse)
            grad_probs = dot_tt(vs[here, :], grad, ((1,), (1,)))
            grad_scores = (probs * (grad_probs - delta)).astype(BF)
            dv[here, :] += jnp.dot(probs.astype(BF), grad, preferred_element_type=F32)
            dk[here, :] += jnp.dot(grad_scores, query, preferred_element_type=F32)
            return acc + dot_tt(kt[:, here], grad_scores, ((1,), (0,)))

        acc = lax.fori_loop(first_tile[i], i + 1, key_tile, jnp.zeros((HEAD, TILE), F32))
        dq[at, :] = acc.T * 0.125
        return 0

    lax.fori_loop(0, SEQ // TILE, query_tile, 0)
    close_blocks(order, dq, grads, 0)
    close_blocks(order, dk, grads, 1)
    close_blocks(order, dv, grads, 2)


def attend_back(order, bounds, first_tile, qkv, grad_in, kept):
    return pl.pallas_call(
        attend_back_body,
        out_shape=jax.ShapeDtypeStruct((16, 3, HALF, 2 * HEAD), BF),
        in_specs=[smem_spec()] * 3 + [vmem_spec()] * 3,
        out_specs=vmem_spec(),
        scratch_shapes=[pltpu.VMEM((SEQ, HEAD), BF)] * 4
        + [pltpu.VMEM((HEAD, SEQ), BF)]
        + [pltpu.VMEM((SEQ, HEAD), F32)] * 3,
        compiler_params=pltpu.CompilerParams(vmem_limit_bytes=VMEM_BYTES),
    )(order, bounds, first_tile, qkv, grad_in, kept)


def experts_body(
    own, tokens, cots, weights, mids, outs, grads,
    pick, pick_t, rows_in, rows_cot, gate_rows, outs_slots, mids_slots,
):
    j = pl.program_id(0)
    lane = lax.broadcasted_iota(jnp.int32, (1, 128), 1)

    @pl.when(j == 0)
    def _():
        def source(s, _):
            at = pl.ds(pl.multiple_of(s * TOK, 16), TOK)
            slots = cots[at, D:WIDE].astype(F32)
            slots_t = slots.T
            slot_at = lax.broadcasted_iota(jnp.int32, (CAP, TOK), 0).astype(F32)
            parts = []
            for n in range(EXP_DEV):
                wanted = own[0] * EXP_DEV + n
                rows_at = lax.broadcasted_iota(jnp.int32, (128, TOK), 0)
                line = jnp.sum(
                    jnp.where(rows_at == wanted, slots_t, 0.0), axis=0, keepdims=True
                )
                parts.append(jnp.where(slot_at == line, 1.0, 0.0))
            chosen = jnp.concatenate(parts, axis=0)
            pick[s] = chosen.astype(BF)
            pick_t[s] = chosen.T.astype(BF)
            moved = jnp.dot(pick[s], tokens[at, :], preferred_element_type=F32)
            turned = jnp.dot(pick[s], cots[at, 0:D], preferred_element_type=F32)
            for n in range(EXP_DEV):
                here = pl.ds(pl.multiple_of(s * CAP, 16), CAP)
                part = slice(n * CAP, (n + 1) * CAP)
                rows_in[n, here, :] = moved[part, 0:D].astype(BF)
                rows_cot[n, here, :] = turned[part].astype(BF)
                wanted = own[0] * EXP_DEV + n
                gate = jnp.sum(
                    jnp.where((lane == wanted) | (lane == wanted + EXPERTS), moved[part, D:WIDE], 0.0),
                    axis=1,
                    keepdims=True,
                )
                gate_rows[n, here, :] = jnp.broadcast_to(gate, (CAP, 128))
            return 0

        lax.fori_loop(0, 8, source, 0)

    w_in = weights[0, :, 0:64, :].reshape(D, 2 * FF)
    w_out = weights[0, :, 64:96, :].reshape(FF, D)
    x = rows_in[j]
    cot = rows_cot[j].astype(F32)
    gate = gate_rows[j][:, 0:1]
    acts = jnp.dot(x, w_in, preferred_element_type=F32)
    gate_act, up_act = acts[:, 0:FF], acts[:, FF:]
    sig = 1.0 / (1.0 + jnp.exp(-gate_act))
    silu = gate_act * sig
    inner = (silu * up_act).astype(BF)
    result = jnp.dot(inner, w_out, preferred_element_type=F32)
    grad_gate = jnp.sum(cot * result, axis=1, keepdims=True)
    grad_rows = (gate * cot).astype(BF)
    grad_inner = dot_tt(grad_rows, w_out, ((1,), (1,)))
    grad_gate_act = grad_inner * up_act * (sig * (1.0 + gate_act * (1.0 - sig)))
    grad_up_act = grad_inner * silu
    grad_acts = jnp.concatenate([grad_gate_act, grad_up_act], axis=1).astype(BF)
    grad_x = dot_tt(grad_acts, w_in, ((1,), (1,)))
    grads[0, :, 64:96, :] = dot_tt(inner, grad_rows, ((0,), (0,))).astype(BF).reshape(16, 32, D)
    grads[0, :, 0:64, :] = dot_tt(x, grad_acts, ((0,), (0,))).astype(BF).reshape(16, 64, D)
    grad_high = grad_gate.astype(BF).astype(F32)
    wanted = own[0] * EXP_DEV + j
    spread = jnp.where(
        lane == wanted,
        grad_high,
        jnp.where(lane == wanted + EXPERTS, grad_gate - grad_high, 0.0),
    )
    weighted = (gate * result).astype(BF)
    for s in range(8):
        part = slice(s * CAP, (s + 1) * CAP)
        there = pl.ds(pl.multiple_of(j * CAP, 16), CAP)
        outs_slots[s, there, :] = weighted[part]
        mids_slots[s, there, 0:D] = grad_x[part].astype(BF)
        mids_slots[s, there, D:WIDE] = spread[part].astype(BF)

    @pl.when(j == EXP_DEV - 1)
    def _():
        def source(s, _):
            mids[s] = jnp.dot(pick_t[s], mids_slots[s], preferred_element_type=F32).astype(BF)
            outs[s] = jnp.dot(pick_t[s], outs_slots[s], preferred_element_type=F32).astype(BF)
            return 0

        lax.fori_loop(0, 8, source, 0)


def run_experts(tokens, cots, weights):
    own = lax.axis_index("exp").astype(jnp.int32).reshape(1)
    whole = lambda shape: pl.BlockSpec(shape, lambda j: (0,) * len(shape), pipeline_mode=pl.Buffered(1))
    return pl.pallas_call(
        experts_body,
        grid=(EXP_DEV,),
        out_shape=[
            jax.ShapeDtypeStruct((8, TOK, WIDE), BF),
            jax.ShapeDtypeStruct((8, TOK, D), BF),
            jax.ShapeDtypeStruct((4, 16, 96, 1024), BF),
        ],
        in_specs=[
            smem_spec(),
            whole((8 * TOK, WIDE)),
            whole((8 * TOK, WIDE)),
            pl.BlockSpec((1, 16, 96, 1024), lambda j: (j, 0, 0, 0)),
        ],
        out_specs=[
            whole((8, TOK, WIDE)),
            whole((8, TOK, D)),
            pl.BlockSpec((1, 16, 96, 1024), lambda j: (j, 0, 0, 0)),
        ],
        scratch_shapes=[
            pltpu.VMEM((8, TOK, TOK), BF),
            pltpu.VMEM((8, TOK, TOK), BF),
            pltpu.VMEM((EXP_DEV, 8 * CAP, D), BF),
            pltpu.VMEM((EXP_DEV, 8 * CAP, D), BF),
            pltpu.VMEM((EXP_DEV, 8 * CAP, 128), F32),
            pltpu.VMEM((8, TOK, D), BF),
            pltpu.VMEM((8, TOK, WIDE), BF),
        ],
        compiler_params=pltpu.CompilerParams(vmem_limit_bytes=VMEM_BYTES),
    )(own, tokens, cots, weights)


def normed(values, gain_vec):
    return values * lax.rsqrt(jnp.mean(values * values, axis=-1, keepdims=True) + EPS) * gain_vec


def angles(positions):
    half_width = HEAD // 2
    freqs = 10000.0 ** (-2.0 * jnp.arange(half_width, dtype=F32) / HEAD)
    turned = positions.astype(F32)[:, None] * freqs[None, :]
    return (jnp.cos(turned), jnp.sin(turned))


def rotate(values, cosine, sine):
    half_width = values.shape[-1] // 2
    first_half = values[..., :half_width]
    second = values[..., half_width:]
    return jnp.concatenate(
        [first_half * cosine - second * sine, second * cosine + first_half * sine], axis=-1
    )


def slot_matrix(routes, priority):
    hit = (routes[:, :, None] == jnp.arange(EXPERTS, dtype=jnp.int32)).astype(BF)
    before = (priority[None, :] < priority[:, None]).astype(BF)
    inside = jnp.dot(before, hit.reshape(TOK, TOP * EXPERTS), preferred_element_type=F32)
    inside = inside.reshape(TOK, TOP, EXPERTS)
    hit = hit.astype(F32)
    counts = jnp.sum(hit, axis=0)
    earlier = jnp.cumsum(counts, axis=0) - counts
    slot = jnp.sum(hit * (inside + earlier[None]), axis=1)
    named = jnp.sum(hit, axis=1)
    return jnp.where((named > 0) & (slot < CAP), slot, -1.0)


def pack_heads(values):
    return values.reshape(2, HALF, HEADS, HEAD).transpose(2, 1, 0, 3).reshape(HEADS, HALF, 2 * HEAD)


def unpack_heads(blocks):
    return blocks.reshape(HEADS, HALF, 2, HEAD).transpose(2, 1, 0, 3).reshape(TOK, HEADS * HEAD)


def twice(values):
    return jnp.repeat(values.reshape(TOK, KV_HEADS, 1, HEAD), 2, axis=2).reshape(TOK, HEADS * HEAD)


def pairs_summed(values):
    return jnp.sum(values.reshape(TOK, KV_HEADS, 2, HEAD), axis=2)


def body(
    hidden_in, cotangent, segments, routes, priority, pair_order, attn_gain, w_query, w_key, w_value,
    query_gain, key_gain, w_output, ffn_gain, w_router, w_gate, w_up, w_down,
):
    gains = jnp.stack(
        [attn_gain, query_gain, jnp.concatenate([key_gain, jnp.zeros((64,), BF)]), ffn_gain], axis=1
    )
    misc = jnp.concatenate([w_router, gains, jnp.zeros((128, 256 - 36), BF)], axis=1)
    slots = slot_matrix(routes[0], priority[0, 0])
    slots_low = jnp.concatenate([slots, jnp.full((TOK, 96), -1.0, F32)], axis=1).astype(BF)
    dense, cots, experts = first_gather(
        w_query, w_key, w_value, w_output, misc, cotangent[0], slots_low, w_gate, w_up, w_down
    )
    qkv_weight = dense[:, 0:2048]
    output_weight = dense[:, 2048:3072]
    router_weight = dense[:, 3072:3104]
    gain_attn = dense[:, 3104].astype(F32)
    gain_query = dense[:, 3105].astype(F32)
    gain_key = dense[:, 3106].reshape(8, 128)[:, :64].reshape(512).astype(F32)
    gain_ffn = dense[:, 3107].astype(F32)

    first_block = pair_order[lax.axis_index("ctx")]
    local = jnp.arange(HALF, dtype=jnp.int32)
    my_positions = jnp.concatenate([first_block * HALF + local, (31 - first_block) * HALF + local])
    seg = segments[0]
    bounds = jnp.sum((seg[None, :] < jnp.arange(1, 4)[:, None]).astype(jnp.int32), axis=1)
    tile_at = jnp.arange(SEQ // TILE, dtype=jnp.int32) * TILE
    first_tile = jnp.max(
        jnp.where(bounds[:, None] <= tile_at[None, :], bounds[:, None], 0), axis=0
    ) // TILE

    resid_in = hidden_in[0].astype(F32)
    normed_in, norm_in_pull = jax.vjp(normed, resid_in, gain_attn)
    normed_low = normed_in.astype(BF)
    projected = jnp.dot(normed_low, qkv_weight, preferred_element_type=F32)
    query_proj, key_proj = projected[:, 0:1024], projected[:, 1024:1536]
    value_low = projected[:, 1536:2048].astype(BF)
    cosine, sine = angles(my_positions)
    cosine, sine = cosine[:, None, :], sine[:, None, :]

    def shape_query(projected, gain_vec):
        return rotate(normed(projected, gain_vec).reshape(TOK, HEADS, HEAD), cosine, sine)

    def shape_key(projected, gain_vec):
        return rotate(normed(projected, gain_vec).reshape(TOK, KV_HEADS, HEAD), cosine, sine)

    query_rot, query_pull = jax.vjp(shape_query, query_proj, gain_query)
    key_rot, key_pull = jax.vjp(shape_key, key_proj, gain_key)
    sent = jnp.stack(
        [
            pack_heads(query_rot.astype(BF)),
            pack_heads(twice(key_rot.astype(BF))),
            pack_heads(twice(value_low)),
        ],
        axis=1,
    )
    qkv = exchange(sent, 5)
    head_out, kept = attend(pair_order, bounds, first_tile, qkv)
    attended = unpack_heads(exchange(head_out, 6)[:, 0])

    after_attn = resid_in + jnp.dot(attended, output_weight, preferred_element_type=F32)
    normed_mid, norm_mid_pull = jax.vjp(normed, after_attn, gain_ffn)
    mid_low = normed_mid.astype(BF)
    logits = jnp.dot(mid_low, router_weight, preferred_element_type=F32)
    soft = jax.nn.softmax(logits, axis=-1)
    gates = jnp.where(slots >= 0, soft, 0.0)
    gates_high = gates.astype(BF)
    gates_low = (gates - gates_high.astype(F32)).astype(BF)
    tokens = tokens_gather(
        jnp.concatenate([mid_low, gates_high, gates_low, jnp.zeros((TOK, 64), BF)], axis=1)
    )
    mid_parts, out_parts, expert_grads = run_experts(tokens, cots, experts)
    mid, out = combine(mid_parts, out_parts)
    layer_out = after_attn + out

    grad_top = cotangent[0].astype(F32)
    grad_gates = mid[:, D : D + EXPERTS] + mid[:, D + EXPERTS : D + 2 * EXPERTS]
    grad_logits = soft * (grad_gates - jnp.sum(soft * grad_gates, axis=-1, keepdims=True))
    grad_mid = mid[:, 0:D] + jnp.dot(grad_logits, router_weight.astype(F32).T, precision=HIGH)
    grad_router = jnp.dot(mid_low.astype(F32).T, grad_logits, precision=HIGH)
    grad_after_norm, grad_ffn_gain = norm_mid_pull(grad_mid)
    grad_after = grad_top + grad_after_norm
    grad_branch = grad_after.astype(BF)
    grad_output = jnp.einsum("te,td->ed", attended, grad_branch, preferred_element_type=F32)
    grad_attended = jnp.einsum(
        "td,ed->te", grad_branch, output_weight, preferred_element_type=F32
    ).astype(BF)
    grad_heads = exchange(pack_heads(grad_attended)[:, None], 7)
    grad_qkv = exchange(attend_back(pair_order, bounds, first_tile, qkv, grad_heads, kept), 8)
    grad_query_rot = unpack_heads(grad_qkv[:, 0]).astype(F32).reshape(TOK, HEADS, HEAD)
    grad_key_rot = pairs_summed(unpack_heads(grad_qkv[:, 1]).astype(F32))
    grad_value = pairs_summed(unpack_heads(grad_qkv[:, 2]).astype(F32)).reshape(TOK, 512)
    grad_query_proj, grad_query_gain = query_pull(grad_query_rot)
    grad_key_proj, grad_key_gain = key_pull(grad_key_rot)
    grad_proj = jnp.concatenate([grad_query_proj, grad_key_proj, grad_value], axis=1).astype(BF)
    grad_weights = jnp.einsum("td,te->de", normed_low, grad_proj, preferred_element_type=F32)
    grad_normed = jnp.einsum("te,de->td", grad_proj, qkv_weight, preferred_element_type=F32)
    grad_resid, grad_attn_gain = norm_in_pull(grad_normed)
    grad_input = grad_after + grad_resid

    key_gain_columns = jnp.concatenate(
        [grad_key_gain.reshape(8, 64), jnp.zeros((8, 64), F32)], axis=1
    ).reshape(1024)
    small = jnp.concatenate(
        [
            grad_router,
            jnp.stack([grad_attn_gain, grad_query_gain, key_gain_columns, grad_ffn_gain], axis=1),
            jnp.zeros((1024, 256 - 36), F32),
        ],
        axis=1,
    )
    dense_grads = jnp.concatenate(
        [grad_weights.astype(BF), grad_output.astype(BF), small.astype(BF)], axis=1
    ).reshape(8, 128, PACK)
    expert_sum, dense_sum = last_sum(expert_grads, dense_grads)
    total = dense_sum.astype(F32)
    return (
        layer_out[None],
        grad_input[None],
        total[:, 3104],
        total[:, 0:1024],
        total[:, 1024:1536],
        total[:, 1536:2048],
        total[:, 3105],
        total[0:64, 3106],
        total[:, 2048:3072],
        total[:, 3107],
        total[:, 3072:3104],
        expert_sum[:, 0:64, 0:FF],
        expert_sum[:, 0:64, FF:],
        expert_sum[:, 64:96, :],
    )


def solution(mesh):
    exp, tok = P("exp"), P("exp", "ctx", None)
    rows = P("exp", None)
    return jax.shard_map(
        body,
        mesh=mesh,
        in_specs=(
            tok, tok, rows, tok, tok, P(), exp, rows, rows, rows, exp, exp, rows, exp, rows,
            tok, tok, tok,
        ),
        out_specs=(
            tok, tok, exp, rows, rows, rows, exp, exp, rows, exp, rows, tok, tok, tok,
        ),
        check_vma=False,
    )
```

```python
import functools

import jax
import jax.numpy as jnp
from jax import lax
from jax.experimental import pallas as pl
from jax.experimental.pallas import tpu as pltpu
from jax.sharding import PartitionSpec as P

MESH = pl.DeviceIdType.MESH
BF = jnp.bfloat16
F32 = jnp.float32
HEADS = 16
KV_HEADS = 8
HEAD = 64
TOP = 8
EXP_DEV = 4
EXPERTS = 32
TOK = 192
HALF = 96
D = 1024
FF = 512
CAP = 48
SEQ = 3072
TILE = 256
WIDE = D + 128
PACK = 3328
EPS = 1e-06
HIGH = lax.Precision.HIGHEST
MASKED = -1e30
VMEM_BYTES = 60 * 1024 * 1024


class Place:
    def __init__(self):
        self.c = lax.axis_index("ctx")
        self.e = lax.axis_index("exp")
        self.x, self.k = self.e // 2, self.e % 2
        self.y, self.z = self.c // 4, self.c % 4

    def exp_at(self, shift):
        return ((self.x + shift) % 4) * 2 + self.k

    def along_x(self, shift):
        return (self.c, self.exp_at(shift))

    def sibling(self):
        return (self.c, self.x * 2 + 1 - self.k)

    def ctx_at(self, half, first, second):
        if half == 0:
            return ((self.y + second) % 4) * 4 + (self.z + first) % 4
        return ((self.y + first) % 4) * 4 + (self.z + second) % 4

    def along_first(self, half, shift):
        return (self.ctx_at(half, shift, 0), self.e)

    def along_second(self, half, shift):
        return (self.ctx_at(half, 0, shift), self.e)

    def ctx_ahead(self, shift):
        return (self.c + shift) % 16


class Mail:
    def __init__(self, send_sems, recv_sems, place):
        self.send_sems, self.recv_sems, self.place = send_sems, recv_sems, place
        self.used, self.sent = 0, []

    def slots(self, number):
        first = self.used
        self.used += number
        return list(range(first, first + number))

    def send(self, slot, src, dst, device):
        copy = pltpu.make_async_remote_copy(
            src_ref=src,
            dst_ref=dst,
            send_sem=self.send_sems.at[slot],
            recv_sem=self.recv_sems.at[slot],
            device_id=device,
            device_id_type=MESH,
        )
        copy.start()
        self.sent.append(copy)

    def wait(self, slot, region):
        pltpu.make_async_remote_copy(
            src_ref=region,
            dst_ref=region,
            send_sem=self.send_sems.at[slot],
            recv_sem=self.recv_sems.at[slot],
            device_id=self.place.sibling(),
            device_id_type=MESH,
        ).wait_recv()

    def finish(self):
        for copy in self.sent:
            copy.wait_send()
        self.sent = []


def meet(devices):
    barrier = pltpu.get_barrier_semaphore()
    for device in devices:
        pl.semaphore_signal(barrier, inc=1, device_id=device, device_id_type=MESH)
    pl.semaphore_wait(barrier, len(devices))


def ring_x_peers(place):
    return [place.along_x(1), place.along_x(3), place.sibling()]


def ring_yz_peers(place):
    return [
        place.along_first(0, 1),
        place.along_first(0, 3),
        place.along_first(1, 1),
        place.along_first(1, 3),
    ]


def ctx_peers(place):
    return [(place.ctx_ahead(shift), place.e) for shift in range(1, 16)]


def interleave(routines):
    routines = list(routines)
    while routines:
        for routine in list(routines):
            try:
                next(routine)
            except StopIteration:
                routines.remove(routine)


def gather_x(place, mail, out, rows):
    (to_right, to_left, to_sib, far0, far1, sib_l, sib_r, sib_f0, sib_f1) = mail.slots(9)
    half = rows // 2

    def shard(shift, core_same=True):
        exp = place.exp_at(shift) if core_same else place.exp_at(shift) + 1 - 2 * place.k
        return out.at[pl.ds(pl.multiple_of(exp * rows, 16), rows)]

    def part(shift, which, core_same=True):
        exp = place.exp_at(shift) if core_same else place.exp_at(shift) + 1 - 2 * place.k
        return out.at[pl.ds(pl.multiple_of(exp * rows + which * half, 16), half)]

    right, left, sib = place.along_x(1), place.along_x(3), place.sibling()
    mail.send(to_right, shard(0), shard(0), right)
    mail.send(to_left, shard(0), shard(0), left)
    mail.send(to_sib, shard(0), shard(0), sib)
    yield
    mail.wait(to_right, shard(3))
    mail.send(far0, part(3, 0), part(3, 0), right)
    mail.send(sib_l, shard(3), shard(3), sib)
    mail.wait(to_left, shard(1))
    mail.send(far1, part(1, 1), part(1, 1), left)
    mail.send(sib_r, shard(1), shard(1), sib)
    yield
    mail.wait(far0, part(2, 0))
    mail.send(sib_f0, part(2, 0), part(2, 0), sib)
    mail.wait(far1, part(2, 1))
    mail.send(sib_f1, part(2, 1), part(2, 1), sib)
    yield
    mail.wait(to_sib, shard(0, False))
    mail.wait(sib_l, shard(3, False))
    mail.wait(sib_r, shard(1, False))
    mail.wait(sib_f0, part(2, 0, False))
    mail.wait(sib_f1, part(2, 1, False))


def gather_yz(place, mail, out, half):
    first, second = (functools.partial(f, half) for f in (place.along_first, place.along_second))

    def piece(a, b):
        return out.at[pl.ds(2 * half, 2), place.ctx_at(half, a, b)]

    def quarter(a, b, which):
        return out.at[2 * half + which, place.ctx_at(half, a, b)]

    f_r, f_l, f_far0, f_far1 = mail.slots(4)
    mail.send(f_r, piece(0, 0), piece(0, 0), first(1))
    mail.send(f_l, piece(0, 0), piece(0, 0), first(3))
    s_slots = {a: mail.slots(2) for a in (0, 1, 3)}
    s_far = {a: mail.slots(2) for a in (0, 1, 2, 3)}
    s_quarters = mail.slots(4)
    mail.send(s_slots[0][0], piece(0, 0), piece(0, 0), second(1))
    mail.send(s_slots[0][1], piece(0, 0), piece(0, 0), second(3))
    yield
    mail.wait(f_r, piece(3, 0))
    mail.send(f_far0, quarter(3, 0, 0), quarter(3, 0, 0), first(1))
    mail.wait(f_l, piece(1, 0))
    mail.send(f_far1, quarter(1, 0, 1), quarter(1, 0, 1), first(3))
    for a in (3, 1):
        mail.send(s_slots[a][0], piece(a, 0), piece(a, 0), second(1))
        mail.send(s_slots[a][1], piece(a, 0), piece(a, 0), second(3))
    yield
    mail.wait(s_slots[0][0], piece(0, 3))
    mail.send(s_far[0][0], quarter(0, 3, 0), quarter(0, 3, 0), second(1))
    mail.wait(s_slots[0][1], piece(0, 1))
    mail.send(s_far[0][1], quarter(0, 1, 1), quarter(0, 1, 1), second(3))
    mail.wait(f_far0, quarter(2, 0, 0))
    mail.send(s_quarters[0], quarter(2, 0, 0), quarter(2, 0, 0), second(1))
    mail.send(s_quarters[1], quarter(2, 0, 0), quarter(2, 0, 0), second(3))
    mail.wait(f_far1, quarter(2, 0, 1))
    mail.send(s_quarters[2], quarter(2, 0, 1), quarter(2, 0, 1), second(1))
    mail.send(s_quarters[3], quarter(2, 0, 1), quarter(2, 0, 1), second(3))
    yield
    for a in (3, 1):
        mail.wait(s_slots[a][0], piece(a, 3))
        mail.send(s_far[a][0], quarter(a, 3, 0), quarter(a, 3, 0), second(1))
        mail.wait(s_slots[a][1], piece(a, 1))
        mail.send(s_far[a][1], quarter(a, 1, 1), quarter(a, 1, 1), second(3))
    yield
    mail.wait(s_quarters[0], quarter(2, 3, 0))
    mail.send(s_far[2][0], quarter(2, 3, 0), quarter(2, 3, 0), second(1))
    mail.wait(s_quarters[3], quarter(2, 1, 1))
    mail.send(s_far[2][1], quarter(2, 1, 1), quarter(2, 1, 1), second(3))
    mail.wait(s_quarters[1], quarter(2, 1, 0))
    mail.wait(s_quarters[2], quarter(2, 3, 1))
    yield
    for a in (0, 1, 2, 3):
        mail.wait(s_far[a][0], quarter(a, 2, 0))
        mail.wait(s_far[a][1], quarter(a, 2, 1))


GATHER_YZ_COPIES = 2 * 22


def add_rows(out, terms, rows, step=16):
    def body(i, _):
        at = pl.ds(pl.multiple_of(i * step, step), step)
        total = terms[0][at].astype(F32)
        for term in terms[1:]:
            total = total + term[at].astype(F32)
        out[at] = total.astype(out.dtype)
        return 0

    lax.fori_loop(0, rows // step, body, 0)


def scatter_x(place, mail, grads, out, sib_buf, sums, near, far, rows, fill=None, extra=None):
    half = rows // 2
    s_sib = mail.slots(4)
    far0, far1, r_free, r_dep, l_free, l_dep = mail.slots(6)
    right, left, sib = place.along_x(1), place.along_x(3), place.sibling()
    order = (2, 1, 3, 0)
    for at, shift in enumerate(order):
        theirs = place.exp_at(shift) + 1 - 2 * place.k
        if fill is not None:
            fill(theirs)
        mail.send(s_sib[at], grads.at[theirs], sib_buf.at[at], sib)
        if fill is not None:
            fill(place.exp_at(shift))
            if at < 3:
                yield
        if fill is not None and at == 0:
            mail.wait(s_sib[0], sib_buf.at[0])
            add_rows(sums.at[0, 0], [grads.at[place.exp_at(2), pl.ds(0, half)], sib_buf.at[0, pl.ds(0, half)]], half)
            mail.send(far0, sums.at[0, 0], far.at[0], right)
            add_rows(sums.at[0, 1], [grads.at[place.exp_at(2), pl.ds(half, half)], sib_buf.at[0, pl.ds(half, half)]], half)
            mail.send(far1, sums.at[0, 1], far.at[1], left)
    yield

    def mine(shift, which):
        return grads.at[place.exp_at(shift), pl.ds(which * half, half)]

    def from_sib(at, which):
        return sib_buf.at[at, pl.ds(which * half, half)]

    if fill is None:
        mail.wait(s_sib[0], sib_buf.at[0])
        add_rows(sums.at[0, 0], [mine(2, 0), from_sib(0, 0)], half)
        mail.send(far0, sums.at[0, 0], far.at[0], right)
        add_rows(sums.at[0, 1], [mine(2, 1), from_sib(0, 1)], half)
        mail.send(far1, sums.at[0, 1], far.at[1], left)
        yield
    mail.wait(s_sib[1], sib_buf.at[1])
    add_rows(sums.at[1, 1], [mine(1, 1), from_sib(1, 1)], half)
    mail.send(r_free, sums.at[1, 1], near.at[0, 1], right)
    mail.wait(s_sib[2], sib_buf.at[2])
    add_rows(sums.at[2, 0], [mine(3, 0), from_sib(2, 0)], half)
    mail.send(l_free, sums.at[2, 0], near.at[1, 0], left)
    yield
    mail.wait(far0, far.at[0])
    add_rows(sums.at[1, 0], [mine(1, 0), from_sib(1, 0), far.at[0]], half)
    mail.send(r_dep, sums.at[1, 0], near.at[0, 0], right)
    mail.wait(far1, far.at[1])
    add_rows(sums.at[2, 1], [mine(3, 1), from_sib(2, 1), far.at[1]], half)
    mail.send(l_dep, sums.at[2, 1], near.at[1, 1], left)
    yield
    mail.wait(s_sib[3], sib_buf.at[3])
    mail.wait(r_free, near.at[0, 1])
    mail.wait(l_free, near.at[1, 0])
    mail.wait(r_dep, near.at[0, 0])
    mail.wait(l_dep, near.at[1, 1])
    for which in (0, 1):
        at = pl.ds(which * half, half)
        terms = [mine(0, which), from_sib(3, which), near.at[0, which], near.at[1, which]]
        add_rows(out.at[at], terms + ([] if extra is None else [extra.at[at]]), half)


SCATTER_X_COPIES = 10


def scatter_x_scratch(rows, columns):
    half = rows // 2
    return [
        pltpu.VMEM((4, rows, columns), BF),
        pltpu.VMEM((3, 2, half, columns), BF),
        pltpu.VMEM((2, 2, half, columns), BF),
        pltpu.VMEM((2, half, columns), BF),
    ]


def scatter_yz(place, mail, loads, grads, out, half, far, near, sums, mid, far2, near2, sums2):
    first, second = (functools.partial(f, half) for f in (place.along_first, place.along_second))
    rows = grads.shape[2]

    def quarter(a, b, which):
        return grads.at[2 * half + which, place.ctx_at(half, a, b)]

    order = (2, 1, 3, 0)
    own = []
    for at, a in enumerate(order):
        for n, (src, dst) in enumerate(
            (
                (quarter(a, 1, 0), sums.at[half, 0, at]),
                (quarter(a, 3, 1), sums.at[half, 1, at]),
                (quarter(a, 0, 0), mid.at[half, 0, at]),
                (quarter(a, 0, 1), mid.at[half, 1, at]),
            )
        ):
            own.append(pltpu.make_async_copy(src, dst, loads.at[half * 16 + at * 4 + n]))
            own[-1].start()
    sl_far = {a: mail.slots(2) for a in order}
    sl_free = {a: mail.slots(2) for a in order}
    sl_dep = {a: mail.slots(2) for a in order}
    for at, a in enumerate(order):
        mail.send(sl_far[a][0], quarter(a, 2, 0), far.at[half, 0, at], second(1))
        mail.send(sl_far[a][1], quarter(a, 2, 1), far.at[half, 1, at], second(3))
    for at, a in enumerate(order):
        mail.send(sl_free[a][0], quarter(a, 1, 1), near.at[half, 0, 1, at], second(1))
        mail.send(sl_free[a][1], quarter(a, 3, 0), near.at[half, 1, 0, at], second(3))
    yield
    for copy in own:
        copy.wait()
    for at, a in enumerate(order):
        mail.wait(sl_far[a][0], far.at[half, 0, at])
        add_rows(sums.at[half, 0, at], [sums.at[half, 0, at], far.at[half, 0, at]], rows)
        mail.send(sl_dep[a][0], sums.at[half, 0, at], near.at[half, 0, 0, at], second(1))
        mail.wait(sl_far[a][1], far.at[half, 1, at])
        add_rows(sums.at[half, 1, at], [sums.at[half, 1, at], far.at[half, 1, at]], rows)
        mail.send(sl_dep[a][1], sums.at[half, 1, at], near.at[half, 1, 1, at], second(3))
        yield
    m_far, m_free, m_dep = mail.slots(2), mail.slots(2), mail.slots(2)
    for at, a in enumerate(order):
        mail.wait(sl_free[a][0], near.at[half, 0, 1, at])
        mail.wait(sl_free[a][1], near.at[half, 1, 0, at])
        mail.wait(sl_dep[a][0], near.at[half, 0, 0, at])
        mail.wait(sl_dep[a][1], near.at[half, 1, 1, at])
        for which in (0, 1):
            add_rows(
                mid.at[half, which, at],
                [mid.at[half, which, at], near.at[half, 0, which, at], near.at[half, 1, which, at]],
                rows,
            )
        if a == 2:
            mail.send(m_far[0], mid.at[half, 0, at], far2.at[half, 0], first(1))
            mail.send(m_far[1], mid.at[half, 1, at], far2.at[half, 1], first(3))
        if a == 1:
            mail.send(m_free[0], mid.at[half, 1, at], near2.at[half, 0, 1], first(1))
        if a == 3:
            mail.send(m_free[1], mid.at[half, 0, at], near2.at[half, 1, 0], first(3))
        yield
    mail.wait(m_far[0], far2.at[half, 0])
    add_rows(sums2.at[half, 0], [mid.at[half, 0, 1], far2.at[half, 0]], rows)
    mail.send(m_dep[0], sums2.at[half, 0], near2.at[half, 0, 0], first(1))
    mail.wait(m_far[1], far2.at[half, 1])
    add_rows(sums2.at[half, 1], [mid.at[half, 1, 2], far2.at[half, 1]], rows)
    mail.send(m_dep[1], sums2.at[half, 1], near2.at[half, 1, 1], first(3))
    yield
    mail.wait(m_free[0], near2.at[half, 0, 1])
    mail.wait(m_free[1], near2.at[half, 1, 0])
    mail.wait(m_dep[0], near2.at[half, 0, 0])
    mail.wait(m_dep[1], near2.at[half, 1, 1])
    for which in (0, 1):
        add_rows(
            out.at[2 * half + which],
            [mid.at[half, which, 3], near2.at[half, 0, which], near2.at[half, 1, which]],
            rows,
        )


SCATTER_YZ_COPIES = 2 * 30


def scatter_yz_scratch(rows, columns):
    one = (rows, columns)
    return [
        pltpu.SemaphoreType.DMA((32,)),
        pltpu.VMEM((2, 2, 4) + one, BF),
        pltpu.VMEM((2, 2, 2, 4) + one, BF),
        pltpu.VMEM((2, 2, 4) + one, BF),
        pltpu.VMEM((2, 2, 4) + one, BF),
        pltpu.VMEM((2, 2) + one, BF),
        pltpu.VMEM((2, 2, 2) + one, BF),
        pltpu.VMEM((2, 2) + one, BF),
    ]


SUM_ROWS = 16
SUM_COLUMNS = PACK // 2


def sum_ctx(place, mail, mine, out, slots):
    up, down = mail.slots(15), mail.slots(15)

    def piece(ref, c):
        return ref.at[
            pl.ds(pl.multiple_of((c // 2) * SUM_ROWS, SUM_ROWS), SUM_ROWS),
            pl.ds(pl.multiple_of((c % 2) * SUM_COLUMNS, 128), SUM_COLUMNS),
        ]

    for shift in range(1, 16):
        c = place.ctx_ahead(shift)
        mail.send(up[shift - 1], piece(mine, c), slots.at[shift], (c, place.e))
    yield
    for shift in range(1, 16):
        mail.wait(up[shift - 1], slots.at[shift])
    total = piece(mine, place.c)[...].astype(F32)
    for shift in range(1, 16):
        total = total + slots[shift].astype(F32)
    own = piece(out, place.c)
    own[...] = total.astype(BF)
    for shift in range(1, 16):
        c = place.ctx_ahead(shift)
        mail.send(down[shift - 1], own, own, (c, place.e))
    yield
    for shift in range(1, 16):
        mail.wait(down[shift - 1], piece(out, place.ctx_ahead(16 - shift)))


def any_spec():
    return pl.BlockSpec(memory_space=pl.ANY)


def vmem_spec():
    return pl.BlockSpec(memory_space=pltpu.VMEM)


def sends(body, number, outs, args, in_specs, out_specs, scratch, collective_id):
    return pl.pallas_call(
        body,
        out_shape=outs,
        in_specs=in_specs,
        out_specs=out_specs,
        scratch_shapes=list(scratch)
        + [pltpu.SemaphoreType.DMA((number,)), pltpu.SemaphoreType.DMA((number,))],
        compiler_params=pltpu.CompilerParams(
            collective_id=collective_id, has_side_effects=True, vmem_limit_bytes=VMEM_BYTES
        ),
    )(*args)


def pack_pair(sent, kind, heads, low, high):
    one, two = swap_pair(low, high)
    for head in heads[0]:
        sent[head, kind] = one.astype(BF)
    for head in heads[1]:
        sent[head, kind] = two.astype(BF)


def swap_heads(place, mail, sent, arrived):
    slots = mail.slots(15)
    for shift in range(1, 16):
        c = place.ctx_ahead(shift)
        mail.send(slots[shift - 1], sent.at[c], arrived.at[place.c], (c, place.e))
    arrived[place.c] = sent[place.c]
    yield
    for shift in range(1, 16):
        mail.wait(slots[shift - 1], arrived.at[place.ctx_ahead(16 - shift)])


def first_body(
    w_query, w_key, w_value, w_output, misc, cot, slots, w_gate, w_up, hidden, cosine, sine,
    dense_out, cots, w_in, qkv, proj, normed_low, gains, router,
    dense, sent, local_sems, send_sems, recv_sems,
):
    place = Place()
    mail = Mail(send_sems, recv_sems, place)
    tok = pl.ds(pl.multiple_of(place.e * TOK, TOK), TOK)
    pairs = [
        (w_gate, w_in.at[:, place.c, :, pl.ds(0, FF)]),
        (w_up, w_in.at[:, place.c, :, pl.ds(FF, FF)]),
        (cot, cots.at[tok, pl.ds(0, D)]),
        (slots, cots.at[tok, pl.ds(D, 128)]),
    ]
    copies = [
        pltpu.make_async_copy(src, dst, local_sems.at[i]) for i, (src, dst) in enumerate(pairs)
    ]
    for copy in copies:
        copy.start()
    row = pl.ds(pl.multiple_of(place.e * 128, 128), 128)
    dense[row, 0:1024] = w_query[...]
    dense[row, 1024:1536] = w_key[...]
    dense[row, 1536:2048] = w_value[...]
    dense[row, 2048:3072] = w_output[...]
    dense[row, 3072:PACK] = misc[...]
    for copy in copies:
        copy.wait()
    meet(ring_x_peers(place) + ctx_peers(place))

    def main():
        yield from gather_x(place, mail, dense, 128)
        keep = pltpu.make_async_copy(dense, dense_out, local_sems.at[4])
        keep.start()
        cots_gather = gather_x(place, mail, cots, TOK)
        next(cots_gather)
        router[...] = jnp.zeros_like(router)
        gains[...] = jnp.zeros_like(gains)
        for e in range(8):
            at = slice(e * 128, e * 128 + 128)
            block = dense[e * 128 : e * 128 + 48, 3072:3200].astype(F32)
            router[0:32, at] = block[0:32].astype(BF)
            router[32:64, at] = block[0:32].astype(BF)
            gains[0:2, at] = block[32:34]
            gains[2:3, e * 64 : e * 64 + 64] = block[34:35, 0:64]
            gains[3:4, at] = block[35:36]
        values = hidden[...].astype(F32)
        normed_low[...] = (values * rms_rows(values) * gains[0:1, :]).astype(BF)
        for n in range(4):
            at = slice(n * 512, n * 512 + 512)
            proj[:, at] = jnp.dot(normed_low[...], dense[:, at], preferred_element_type=F32)
        query_scale = rms_rows(proj[:, 0:1024])
        key_scale = rms_rows(proj[:, 1024:1536])
        low, high = slice(0, HALF), slice(HALF, TOK)
        for g in range(8):
            at = slice(g * 128, g * 128 + 128)
            values = proj[:, at] * query_scale * gains[1:2, at]
            pack_pair(
                sent, 0, ((2 * g,), (2 * g + 1,)),
                turn_pair(values[low], cosine[low, :], sine[low, :]),
                turn_pair(values[high], cosine[high, :], sine[high, :]),
            )
        for g in range(4):
            at = slice(1024 + g * 128, 1024 + g * 128 + 128)
            heads = ((4 * g, 4 * g + 1), (4 * g + 2, 4 * g + 3))
            values = proj[:, at] * key_scale * gains[2:3, g * 128 : g * 128 + 128]
            pack_pair(
                sent, 1, heads,
                turn_pair(values[low], cosine[low, :], sine[low, :]),
                turn_pair(values[high], cosine[high, :], sine[high, :]),
            )
            at = slice(1536 + g * 128, 1536 + g * 128 + 128)
            pack_pair(sent, 2, heads, proj[low, at], proj[high, at])
        yield from swap_heads(place, mail, sent, qkv)
        yield
        yield from cots_gather
        keep.wait()

    interleave([gather_yz(place, mail, w_in, 0), gather_yz(place, mail, w_in, 1), main()])
    mail.finish()


def first_gather(*args):
    return sends(
        first_body,
        GATHER_YZ_COPIES + 18 + 15,
        [
            jax.ShapeDtypeStruct((1024, PACK), BF),
            jax.ShapeDtypeStruct((8 * TOK, WIDE), BF),
            jax.ShapeDtypeStruct((4, 16, 64, 1024), BF),
            jax.ShapeDtypeStruct((16, 3, HALF, 128), BF),
            jax.ShapeDtypeStruct((TOK, 2048), F32),
            jax.ShapeDtypeStruct((TOK, D), BF),
            jax.ShapeDtypeStruct((8, D), F32),
            jax.ShapeDtypeStruct((128, D), BF),
        ],
        args,
        [vmem_spec()] * 12,
        [any_spec()] * 3 + [vmem_spec()] * 5,
        [
            pltpu.VMEM((1024, PACK), BF),
            pltpu.VMEM((16, 3, HALF, 128), BF),
            pltpu.SemaphoreType.DMA((5,)),
        ],
        1,
    )


def middle_body(
    heads, hidden, gains, router, slots, w_down, dense,
    attended, after, mid_low, soft, tokens, w_out,
    weight, arrived, mine, local_sems, send_sems, recv_sems,
):
    place = Place()
    mail = Mail(send_sems, recv_sems, place)
    load = pltpu.make_async_copy(dense.at[:, pl.ds(2048, 1024)], weight, local_sems.at[0])
    load.start()
    own = pltpu.make_async_copy(w_down, w_out.at[:, place.c], local_sems.at[1])
    own.start()
    own.wait()
    meet(ring_x_peers(place) + ctx_peers(place))

    def main():
        yield from swap_heads(place, mail, heads, arrived)
        for g in range(8):
            at = slice(g * 128, g * 128 + 128)
            low, high = swap_pair(arrived[2 * g, 0].astype(F32), arrived[2 * g + 1, 0].astype(F32))
            attended[0:HALF, at] = low.astype(BF)
            attended[HALF:TOK, at] = high.astype(BF)
        load.wait()
        values = hidden[...].astype(F32) + jnp.dot(
            attended[...], weight[...], preferred_element_type=F32
        )
        after[...] = values
        mid_low[...] = (values * rms_rows(values) * gains[3:4, :]).astype(BF)
        logits = dot_tt(mid_low[...], router[...], ((1,), (1,)))
        lane = lane_of((TOK, 128))
        known = lane < EXPERTS
        peak = jnp.max(jnp.where(known, logits, MASKED), axis=1, keepdims=True)
        weights = jnp.exp(jnp.where(lane < 2 * EXPERTS, logits, MASKED) - peak)
        probs = weights / jnp.sum(jnp.where(known, weights, 0.0), axis=1, keepdims=True)
        soft[...] = probs
        gates = jnp.where(slots[...].astype(F32) >= 0, probs, 0.0)
        gates_high = gates.astype(BF).astype(F32)
        mine[:, 0:D] = mid_low[...]
        mine[:, D:WIDE] = jnp.where(known, gates_high, gates - gates_high).astype(BF)
        place_rows = pltpu.make_async_copy(
            mine, tokens.at[pl.ds(pl.multiple_of(place.e * TOK, TOK), TOK)], local_sems.at[2]
        )
        place_rows.start()
        place_rows.wait()
        yield from gather_x(place, mail, tokens, TOK)

    interleave([main(), gather_yz(place, mail, w_out, 0), gather_yz(place, mail, w_out, 1)])
    mail.finish()


def middle(*args):
    return sends(
        middle_body,
        GATHER_YZ_COPIES + 9 + 15,
        [
            jax.ShapeDtypeStruct((TOK, D), BF),
            jax.ShapeDtypeStruct((TOK, D), F32),
            jax.ShapeDtypeStruct((TOK, D), BF),
            jax.ShapeDtypeStruct((TOK, 128), F32),
            jax.ShapeDtypeStruct((8 * TOK, WIDE), BF),
            jax.ShapeDtypeStruct((4, 16, 32, 1024), BF),
        ],
        args,
        [vmem_spec()] * 6 + [any_spec()],
        [vmem_spec()] * 4 + [any_spec()] * 2,
        [
            pltpu.VMEM((D, D), BF),
            pltpu.VMEM((16, 1, HALF, 128), BF),
            pltpu.VMEM((TOK, WIDE), BF),
            pltpu.SemaphoreType.DMA((3,)),
        ],
        2,
    )


def turn_back_body(
    mids, after, mid_low, soft, cot, gains, router, dense, grads_out,
    grad_after, branch, ffn_grad, router_grad, grad_heads, out_sum,
    *rest,
):
    yz, x = rest[0:8], rest[8:12]
    mid, weight, sent, load_sem, send_sems, recv_sems = rest[12:]
    place = Place()
    mail = Mail(send_sems, recv_sems, place)
    load = pltpu.make_async_copy(dense.at[:, pl.ds(2048, 1024)], weight, load_sem)
    load.start()
    meet(ring_x_peers(place) + ctx_peers(place))

    def main():
        yield from scatter_x(place, mail, mids, mid, *x, TOK)
        lane = lane_of((TOK, 128))
        known = lane < EXPERTS
        halves = mid[:, D:WIDE]
        gate_grads = jnp.where(known, halves + pltpu.roll(halves, 96, 1), 0.0)
        probs = jnp.where(known, soft[...], 0.0)
        grad_logits = probs * (
            gate_grads - jnp.sum(probs * gate_grads, axis=1, keepdims=True)
        )
        high = grad_logits.astype(BF).astype(F32)
        split = (high + pltpu.roll(grad_logits - high, EXPERTS, 1)).astype(BF)
        grad_mid = mid[:, 0:D] + jnp.dot(split, router[...], preferred_element_type=F32)
        both = dot_tt(split, mid_low[...], ((0,), (0,)))
        router_grad[...] = both[0:EXPERTS] + both[EXPERTS : 2 * EXPERTS]
        values = after[...]
        back, gain_grad = norm_back(values, gains[3:4, :], grad_mid, rms_rows(values))
        ffn_grad[...] = gain_grad
        total = cot[...].astype(F32) + back
        grad_after[...] = total
        branch[...] = total.astype(BF)
        load.wait()
        grad_attended = dot_tt(branch[...], weight[...], ((1,), (1,)))
        for g in range(8):
            at = slice(g * 128, g * 128 + 128)
            pack_pair(
                sent, 0, ((2 * g,), (2 * g + 1,)), grad_attended[0:HALF, at], grad_attended[HALF:TOK, at]
            )
        yield from swap_heads(place, mail, sent, grad_heads)

    interleave(
        [
            main(),
            scatter_yz(place, mail, yz[0], grads_out, out_sum, 0, *yz[1:]),
            scatter_yz(place, mail, yz[0], grads_out, out_sum, 1, *yz[1:]),
        ]
    )
    mail.finish()


def turn_back(*args):
    return sends(
        turn_back_body,
        SCATTER_YZ_COPIES + SCATTER_X_COPIES + 15,
        [
            jax.ShapeDtypeStruct((TOK, D), F32),
            jax.ShapeDtypeStruct((TOK, D), BF),
            jax.ShapeDtypeStruct((1, D), F32),
            jax.ShapeDtypeStruct((EXPERTS, D), F32),
            jax.ShapeDtypeStruct((16, 1, HALF, 128), BF),
            jax.ShapeDtypeStruct((4, 32, 1024), F32),
        ],
        args,
        [vmem_spec()] * 7 + [any_spec()] * 2,
        [vmem_spec()] * 6,
        scatter_yz_scratch(32, 1024)
        + scatter_x_scratch(TOK, WIDE)
        + [
            pltpu.VMEM((TOK, WIDE), F32),
            pltpu.VMEM((D, D), BF),
            pltpu.VMEM((16, 1, HALF, 128), BF),
            pltpu.SemaphoreType.DMA,
        ],
        3,
    )


def dot_tt(a, b, dims):
    return lax.dot_general(a, b, (dims, ((), ())), preferred_element_type=F32)


def lane_of(shape):
    return lax.broadcasted_iota(jnp.int32, shape, len(shape) - 1)


def turn_pair(values, cosine, sine):
    first = lane_of(values.shape) % HEAD < HEAD // 2
    other = jnp.where(first, pltpu.roll(values, 96, 1), pltpu.roll(values, 32, 1))
    return values * cosine + other * sine


def swap_pair(one, two):
    low = lane_of(one.shape) < HEAD
    return (
        jnp.where(low, one, pltpu.roll(two, HEAD, 1)),
        jnp.where(low, pltpu.roll(one, HEAD, 1), two),
    )


def norm_back(values, gain, grad, scale_rows):
    inner = jnp.mean(values * gain * grad, axis=1, keepdims=True)
    back = scale_rows * gain * grad - values * (scale_rows * scale_rows * scale_rows * inner)
    return back, jnp.sum(grad * values * scale_rows, axis=0, keepdims=True)


def rms_rows(values):
    return lax.rsqrt(jnp.mean(values * values, axis=1, keepdims=True) + EPS)


def last_body(
    heads, proj, normed_low, attended, branch, after, hidden, cosine, sine, gains, ffn_grad, router_grad,
    after_attn, outs, dense, grads_in,
    in_sum, dense_sum, grad_input, layer_out,
    *rest,
):
    yz, x_outs, x = rest[0:8], rest[8:12], rest[12:16]
    (mine, slots, dense_grads, weight, weight_sem, arrived, turned, grad_proj, gain_rows,
     send_sems, recv_sems) = rest[16:]
    place = Place()
    mail = Mail(send_sems, recv_sems, place)
    load = pltpu.make_async_copy(dense.at[:, pl.ds(0, 2048)], weight, weight_sem)
    load.start()
    meet(ring_x_peers(place) + ctx_peers(place))

    def dense_part():
        yield from swap_heads(place, mail, heads, arrived)

        def query_pair(g, _):
            at = pl.ds(pl.multiple_of(g * 128, 128), 128)
            parts = swap_pair(arrived[2 * g, 0].astype(F32), arrived[2 * g + 1, 0].astype(F32))
            for which in (0, 1):
                rows = pl.ds(which * HALF, HALF)
                turned[rows, at] = turn_pair(parts[which], cosine[rows, :], -sine[rows, :])
            return 0

        lax.fori_loop(0, 8, query_pair, 0)

        def key_pair(g, _):
            at = pl.ds(pl.multiple_of(g * 128, 128), 128)
            for kind in (1, 2):
                parts = swap_pair(
                    arrived[4 * g, kind].astype(F32) + arrived[4 * g + 1, kind].astype(F32),
                    arrived[4 * g + 2, kind].astype(F32) + arrived[4 * g + 3, kind].astype(F32),
                )
                for which in (0, 1):
                    rows = pl.ds(which * HALF, HALF)
                    if kind == 1:
                        turned[rows, pl.ds(pl.multiple_of(1024 + g * 128, 128), 128)] = turn_pair(
                            parts[which], cosine[rows, :], -sine[rows, :]
                        )
                    else:
                        grad_proj[rows, pl.ds(pl.multiple_of(1536 + g * 128, 128), 128)] = parts[
                            which
                        ].astype(BF)
            return 0

        lax.fori_loop(0, 4, key_pair, 0)
        gain_rows[...] = jnp.zeros_like(gain_rows)
        gain_rows[3:4, :] = ffn_grad[...]
        for n, (start, width) in enumerate(((0, 1024), (1024, 512))):
            at = slice(start, start + width)
            values = proj[:, at]
            back, gain_grad = norm_back(
                values, gains[1 + n : 2 + n, 0:width], turned[:, at], rms_rows(values)
            )
            grad_proj[:, at] = back.astype(BF)
            if n == 0:
                gain_rows[1:2, :] = gain_grad
            else:
                for e in range(8):
                    gain_rows[2:3, e * 128 : e * 128 + 64] = gain_grad[:, e * 64 : e * 64 + 64]
        load.wait()
        grad_normed = dot_tt(grad_proj[...], weight[...], ((1,), (1,)))
        values = hidden[...].astype(F32)
        back, gain_grad = norm_back(values, gains[0:1, :], grad_normed, rms_rows(values))
        grad_input[...] = after[...] + back
        gain_rows[0:1, :] = gain_grad

        def fill(e):
            at = pl.ds(pl.multiple_of(e * 128, 128), 128)
            dense_grads[e, :, 0:2048] = dot_tt(normed_low[:, at], grad_proj[...], ((0,), (0,))).astype(BF)
            dense_grads[e, :, 2048:3072] = dot_tt(attended[:, at], branch[...], ((0,), (0,))).astype(BF)
            dense_grads[e, :, 3072:PACK] = jnp.zeros((128, PACK - 3072), BF)
            dense_grads[e, 0:48, 3072:3200] = jnp.concatenate(
                [router_grad[:, at], gain_rows[:, at]], axis=0
            ).astype(BF)

        yield
        yield from scatter_x(place, mail, dense_grads, mine, *x, 128, fill)
        yield from sum_ctx(place, mail, mine, dense_sum, slots)

    def outs_part():
        yield from scatter_x(place, mail, outs, layer_out, *x_outs, TOK, extra=after_attn)

    interleave(
        [
            dense_part(),
            outs_part(),
            scatter_yz(place, mail, yz[0], grads_in, in_sum, 0, *yz[1:]),
            scatter_yz(place, mail, yz[0], grads_in, in_sum, 1, *yz[1:]),
        ]
    )
    mail.finish()


def last_sum(*args):
    return sends(
        last_body,
        SCATTER_YZ_COPIES + 2 * SCATTER_X_COPIES + 45,
        [
            jax.ShapeDtypeStruct((4, 64, 1024), F32),
            jax.ShapeDtypeStruct((128, PACK), BF),
            jax.ShapeDtypeStruct((TOK, D), F32),
            jax.ShapeDtypeStruct((TOK, D), F32),
        ],
        args,
        [vmem_spec()] * 14 + [any_spec()] * 2,
        [vmem_spec()] * 4,
        scatter_yz_scratch(64, 1024)
        + scatter_x_scratch(TOK, D)
        + scatter_x_scratch(128, PACK)
        + [
            pltpu.VMEM((128, PACK), BF),
            pltpu.VMEM((16, SUM_ROWS, SUM_COLUMNS), BF),
            pltpu.VMEM((8, 128, PACK), BF),
            pltpu.VMEM((D, 2048), BF),
            pltpu.SemaphoreType.DMA,
            pltpu.VMEM((16, 3, HALF, 128), BF),
            pltpu.VMEM((TOK, 1536), F32),
            pltpu.VMEM((TOK, 2048), BF),
            pltpu.VMEM((16, 1024), F32),
        ],
        4,
    )


def open_blocks(order, src, which, dst, scale=None):
    def body(c, _):
        block = src[c, which]
        low, high = block[:, 0:HEAD], block[:, HEAD : 2 * HEAD]
        if scale is not None:
            low, high = low * scale, high * scale
        spot = order[c]
        dst[pl.ds(pl.multiple_of(spot * HALF, 16), HALF), :] = low
        dst[pl.ds(pl.multiple_of((31 - spot) * HALF, 16), HALF), :] = high
        return 0

    lax.fori_loop(0, 16, body, 0)


def close_blocks(order, src, dst, which):
    def body(c, _):
        spot = order[c]
        low = src[pl.ds(pl.multiple_of(spot * HALF, 16), HALF), :]
        high = src[pl.ds(pl.multiple_of((31 - spot) * HALF, 16), HALF), :]
        dst[c, which] = jnp.concatenate([low, high], axis=1).astype(dst.dtype)
        return 0

    lax.fori_loop(0, 16, body, 0)


def tile_mask(bounds, i, j):
    query_at = lax.broadcasted_iota(jnp.int32, (1, TILE), 1) + i * TILE
    key_at = lax.broadcasted_iota(jnp.int32, (TILE, TILE), 0) + j * TILE
    start = jnp.zeros((1, TILE), jnp.int32)
    for d in range(3):
        start = jnp.where(query_at >= bounds[d], bounds[d], start)
    return (key_at >= start) & (key_at <= query_at)


def attend_body(order, bounds, first_tile, qkv, attended, kept, qs, ks, vs, vt, outs):
    open_blocks(order, qkv, 0, qs, 0.125)
    open_blocks(order, qkv, 1, ks)
    open_blocks(order, qkv, 2, vs)

    def turn(i, _):
        at = pl.ds(pl.multiple_of(i * TILE, TILE), TILE)
        vt[:, at] = vs[at, :].astype(F32).T.astype(BF)
        return 0

    lax.fori_loop(0, SEQ // TILE, turn, 0)

    def query_tile(i, _):
        at = pl.ds(pl.multiple_of(i * TILE, TILE), TILE)
        query = qs[at, :]

        def key_tile(j, state):
            peak, total, acc = state
            here = pl.ds(pl.multiple_of(j * TILE, TILE), TILE)
            scores = dot_tt(ks[here, :], query, ((1,), (1,)))
            scores = jnp.where(tile_mask(bounds, i, j), scores, MASKED)
            new_peak = jnp.maximum(peak, jnp.max(scores, axis=0, keepdims=True))
            weights = jnp.exp(scores - new_peak)
            keep = jnp.exp(peak - new_peak)
            total = total * keep + jnp.sum(weights, axis=0, keepdims=True)
            acc = acc * keep + dot_tt(vt[:, here], weights.astype(BF), ((1,), (0,)))
            return new_peak, total, acc

        peak, total, acc = lax.fori_loop(
            first_tile[i],
            i + 1,
            key_tile,
            (
                jnp.full((1, TILE), MASKED, F32),
                jnp.zeros((1, TILE), F32),
                jnp.zeros((HEAD, TILE), F32),
            ),
        )
        mixed = acc / total
        kept[0:HEAD, at] = mixed
        kept[HEAD : HEAD + 8, at] = jnp.broadcast_to(peak + jnp.log(total), (8, TILE))
        outs[at, :] = mixed.T
        return 0

    lax.fori_loop(0, SEQ // TILE, query_tile, 0)
    close_blocks(order, outs, attended, 0)


def smem_spec():
    return pl.BlockSpec(memory_space=pltpu.SMEM)


def attend(order, bounds, first_tile, qkv):
    return pl.pallas_call(
        attend_body,
        out_shape=[
            jax.ShapeDtypeStruct((16, 1, HALF, 2 * HEAD), BF),
            jax.ShapeDtypeStruct((HEAD + 8, SEQ), F32),
        ],
        in_specs=[smem_spec()] * 3 + [vmem_spec()],
        out_specs=[vmem_spec()] * 2,
        scratch_shapes=[pltpu.VMEM((SEQ, HEAD), BF)] * 3
        + [pltpu.VMEM((HEAD, SEQ), BF), pltpu.VMEM((SEQ, HEAD), F32)],
        compiler_params=pltpu.CompilerParams(vmem_limit_bytes=VMEM_BYTES),
    )(order, bounds, first_tile, qkv)


def attend_back_body(
    order, bounds, first_tile, qkv, grad_in, kept, grads,
    qs, ks, vs, gs, kt, dq, dk, dv,
):
    open_blocks(order, qkv, 0, qs, 0.125)
    open_blocks(order, qkv, 1, ks)
    open_blocks(order, qkv, 2, vs)
    open_blocks(order, grad_in, 0, gs)
    dk[...] = jnp.zeros_like(dk)
    dv[...] = jnp.zeros_like(dv)

    def turn(i, _):
        at = pl.ds(pl.multiple_of(i * TILE, TILE), TILE)
        kt[:, at] = ks[at, :].astype(F32).T.astype(BF)
        return 0

    lax.fori_loop(0, SEQ // TILE, turn, 0)

    def query_tile(i, _):
        at = pl.ds(pl.multiple_of(i * TILE, TILE), TILE)
        query = qs[at, :]
        grad = gs[at, :]
        mixed = kept[0:HEAD, at]
        lse = kept[HEAD : HEAD + 1, at]
        delta = jnp.sum(mixed * grad.astype(F32).T, axis=0, keepdims=True)

        def key_tile(j, acc):
            here = pl.ds(pl.multiple_of(j * TILE, TILE), TILE)
            scores = dot_tt(ks[here, :], query, ((1,), (1,)))
            scores = jnp.where(tile_mask(bounds, i, j), scores, MASKED)
            probs = jnp.exp(scores - lse)
            grad_probs = dot_tt(vs[here, :], grad, ((1,), (1,)))
            grad_scores = (probs * (grad_probs - delta)).astype(BF)
            dv[here, :] += jnp.dot(probs.astype(BF), grad, preferred_element_type=F32)
            dk[here, :] += jnp.dot(grad_scores, query, preferred_element_type=F32)
            return acc + dot_tt(kt[:, here], grad_scores, ((1,), (0,)))

        acc = lax.fori_loop(first_tile[i], i + 1, key_tile, jnp.zeros((HEAD, TILE), F32))
        dq[at, :] = acc.T * 0.125
        return 0

    lax.fori_loop(0, SEQ // TILE, query_tile, 0)
    close_blocks(order, dq, grads, 0)
    close_blocks(order, dk, grads, 1)
    close_blocks(order, dv, grads, 2)


def attend_back(order, bounds, first_tile, qkv, grad_in, kept):
    return pl.pallas_call(
        attend_back_body,
        out_shape=jax.ShapeDtypeStruct((16, 3, HALF, 2 * HEAD), BF),
        in_specs=[smem_spec()] * 3 + [vmem_spec()] * 3,
        out_specs=vmem_spec(),
        scratch_shapes=[pltpu.VMEM((SEQ, HEAD), BF)] * 4
        + [pltpu.VMEM((HEAD, SEQ), BF)]
        + [pltpu.VMEM((SEQ, HEAD), F32)] * 3,
        compiler_params=pltpu.CompilerParams(vmem_limit_bytes=VMEM_BYTES),
    )(order, bounds, first_tile, qkv, grad_in, kept)


def experts_body(
    own, tokens, cots, weights_in, weights_out, mids, outs, grads_in, grads_out,
    pick, pick_t, rows_in, rows_cot, gate_rows, outs_slots, mids_slots,
):
    j = pl.program_id(0)
    lane = lax.broadcasted_iota(jnp.int32, (1, 128), 1)

    @pl.when(j == 0)
    def _():
        def source(s, _):
            at = pl.ds(pl.multiple_of(s * TOK, 16), TOK)
            slots = cots[at, D:WIDE].astype(F32)
            slots_t = slots.T
            slot_at = lax.broadcasted_iota(jnp.int32, (CAP, TOK), 0).astype(F32)
            parts = []
            for n in range(EXP_DEV):
                wanted = own[0] * EXP_DEV + n
                rows_at = lax.broadcasted_iota(jnp.int32, (128, TOK), 0)
                line = jnp.sum(
                    jnp.where(rows_at == wanted, slots_t, 0.0), axis=0, keepdims=True
                )
                parts.append(jnp.where(slot_at == line, 1.0, 0.0))
            chosen = jnp.concatenate(parts, axis=0)
            pick[s] = chosen.astype(BF)
            pick_t[s] = chosen.T.astype(BF)
            moved = jnp.dot(pick[s], tokens[at, :], preferred_element_type=F32)
            turned = jnp.dot(pick[s], cots[at, 0:D], preferred_element_type=F32)
            for n in range(EXP_DEV):
                here = pl.ds(pl.multiple_of(s * CAP, 16), CAP)
                part = slice(n * CAP, (n + 1) * CAP)
                rows_in[n, here, :] = moved[part, 0:D].astype(BF)
                rows_cot[n, here, :] = turned[part].astype(BF)
                wanted = own[0] * EXP_DEV + n
                gate = jnp.sum(
                    jnp.where((lane == wanted) | (lane == wanted + EXPERTS), moved[part, D:WIDE], 0.0),
                    axis=1,
                    keepdims=True,
                )
                gate_rows[n, here, :] = jnp.broadcast_to(gate, (CAP, 128))
            return 0

        lax.fori_loop(0, 8, source, 0)

    w_in = weights_in[0].reshape(D, 2 * FF)
    w_out = weights_out[0].reshape(FF, D)
    x = rows_in[j]
    cot = rows_cot[j].astype(F32)
    gate = gate_rows[j][:, 0:1]
    acts = jnp.dot(x, w_in, preferred_element_type=F32)
    gate_act, up_act = acts[:, 0:FF], acts[:, FF:]
    sig = 1.0 / (1.0 + jnp.exp(-gate_act))
    silu = gate_act * sig
    inner = (silu * up_act).astype(BF)
    result = jnp.dot(inner, w_out, preferred_element_type=F32)
    grad_gate = jnp.sum(cot * result, axis=1, keepdims=True)
    grad_rows = (gate * cot).astype(BF)
    grad_inner = dot_tt(grad_rows, w_out, ((1,), (1,)))
    grad_gate_act = grad_inner * up_act * (sig * (1.0 + gate_act * (1.0 - sig)))
    grad_up_act = grad_inner * silu
    grad_acts = jnp.concatenate([grad_gate_act, grad_up_act], axis=1).astype(BF)
    grad_x = dot_tt(grad_acts, w_in, ((1,), (1,)))
    grads_out[0] = dot_tt(inner, grad_rows, ((0,), (0,))).astype(BF).reshape(16, 32, D)
    grads_in[0] = dot_tt(x, grad_acts, ((0,), (0,))).astype(BF).reshape(16, 64, D)
    grad_high = grad_gate.astype(BF).astype(F32)
    wanted = own[0] * EXP_DEV + j
    spread = jnp.where(
        lane == wanted,
        grad_high,
        jnp.where(lane == wanted + EXPERTS, grad_gate - grad_high, 0.0),
    )
    weighted = (gate * result).astype(BF)
    for s in range(8):
        part = slice(s * CAP, (s + 1) * CAP)
        there = pl.ds(pl.multiple_of(j * CAP, 16), CAP)
        outs_slots[s, there, :] = weighted[part]
        mids_slots[s, there, 0:D] = grad_x[part].astype(BF)
        mids_slots[s, there, D:WIDE] = spread[part].astype(BF)

    @pl.when(j == EXP_DEV - 1)
    def _():
        def source(s, _):
            mids[s] = jnp.dot(pick_t[s], mids_slots[s], preferred_element_type=F32).astype(BF)
            outs[s] = jnp.dot(pick_t[s], outs_slots[s], preferred_element_type=F32).astype(BF)
            return 0

        lax.fori_loop(0, 8, source, 0)


def run_experts(tokens, cots, w_in, w_out):
    own = lax.axis_index("exp").astype(jnp.int32).reshape(1)
    whole = lambda shape: pl.BlockSpec(shape, lambda j: (0,) * len(shape), pipeline_mode=pl.Buffered(1))
    return pl.pallas_call(
        experts_body,
        grid=(EXP_DEV,),
        out_shape=[
            jax.ShapeDtypeStruct((8, TOK, WIDE), BF),
            jax.ShapeDtypeStruct((8, TOK, D), BF),
            jax.ShapeDtypeStruct((4, 16, 64, 1024), BF),
            jax.ShapeDtypeStruct((4, 16, 32, 1024), BF),
        ],
        in_specs=[
            smem_spec(),
            whole((8 * TOK, WIDE)),
            whole((8 * TOK, WIDE)),
            pl.BlockSpec((1, 16, 64, 1024), lambda j: (j, 0, 0, 0)),
            pl.BlockSpec((1, 16, 32, 1024), lambda j: (j, 0, 0, 0)),
        ],
        out_specs=[
            whole((8, TOK, WIDE)),
            whole((8, TOK, D)),
            pl.BlockSpec((1, 16, 64, 1024), lambda j: (j, 0, 0, 0)),
            pl.BlockSpec((1, 16, 32, 1024), lambda j: (j, 0, 0, 0)),
        ],
        scratch_shapes=[
            pltpu.VMEM((8, TOK, TOK), BF),
            pltpu.VMEM((8, TOK, TOK), BF),
            pltpu.VMEM((EXP_DEV, 8 * CAP, D), BF),
            pltpu.VMEM((EXP_DEV, 8 * CAP, D), BF),
            pltpu.VMEM((EXP_DEV, 8 * CAP, 128), F32),
            pltpu.VMEM((8, TOK, D), BF),
            pltpu.VMEM((8, TOK, WIDE), BF),
        ],
        compiler_params=pltpu.CompilerParams(vmem_limit_bytes=VMEM_BYTES),
    )(own, tokens, cots, w_in, w_out)


def pair_angles(positions):
    half_width = HEAD // 2
    freqs = 10000.0 ** (-2.0 * jnp.arange(half_width, dtype=F32) / HEAD)
    turned = positions.astype(F32)[:, None] * freqs[None, :]
    cosine, sine = jnp.cos(turned), jnp.sin(turned)
    return (
        jnp.concatenate([cosine] * 4, axis=1),
        jnp.concatenate([-sine, sine, -sine, sine], axis=1),
    )


def slot_matrix(routes, priority):
    hit = (routes[:, :, None] == jnp.arange(EXPERTS, dtype=jnp.int32)).astype(BF)
    before = (priority[None, :] < priority[:, None]).astype(BF)
    inside = jnp.dot(before, hit.reshape(TOK, TOP * EXPERTS), preferred_element_type=F32)
    inside = inside.reshape(TOK, TOP, EXPERTS)
    hit = hit.astype(F32)
    counts = jnp.sum(hit, axis=0)
    earlier = jnp.cumsum(counts, axis=0) - counts
    slot = jnp.sum(hit * (inside + earlier[None]), axis=1)
    named = jnp.sum(hit, axis=1)
    return jnp.where((named > 0) & (slot < CAP), slot, -1.0)


def body(
    hidden_in, cotangent, segments, routes, priority, pair_order, attn_gain, w_query, w_key, w_value,
    query_gain, key_gain, w_output, ffn_gain, w_router, w_gate, w_up, w_down,
):
    misc = jnp.concatenate(
        [
            w_router.T,
            jnp.stack(
                [attn_gain, query_gain, jnp.concatenate([key_gain, jnp.zeros((64,), BF)]), ffn_gain]
            ),
            jnp.zeros((128 - 36, 128), BF),
        ]
    )
    misc = jnp.concatenate([misc, jnp.zeros((128, PACK - 3200), BF)], axis=1)
    slots = slot_matrix(routes[0], priority[0, 0])
    slots = jnp.concatenate([slots, slots, jnp.full((TOK, 64), -1.0, F32)], axis=1).astype(BF)

    first_block = pair_order[lax.axis_index("ctx")]
    local = jnp.arange(HALF, dtype=jnp.int32)
    my_positions = jnp.concatenate([first_block * HALF + local, (31 - first_block) * HALF + local])
    cosine, sine = pair_angles(my_positions)
    seg = segments[0]
    bounds = jnp.sum((seg[None, :] < jnp.arange(1, 4)[:, None]).astype(jnp.int32), axis=1)
    tile_at = jnp.arange(SEQ // TILE, dtype=jnp.int32) * TILE
    first_tile = jnp.max(
        jnp.where(bounds[:, None] <= tile_at[None, :], bounds[:, None], 0), axis=0
    ) // TILE

    hidden, cot = hidden_in[0], cotangent[0]
    dense, cots, w_in, qkv, proj, normed_low, gains, router = first_gather(
        w_query, w_key, w_value, w_output, misc, cot, slots, w_gate, w_up, hidden, cosine, sine
    )
    head_out, kept = attend(pair_order, bounds, first_tile, qkv)
    attended, after_attn, mid_low, soft, tokens, w_out = middle(
        head_out, hidden, gains, router, slots, w_down, dense
    )
    mids, outs, grads_in, grads_out = run_experts(tokens, cots, w_in, w_out)
    grad_after, branch, ffn_grad, router_grad, grad_heads, out_sum = turn_back(
        mids, after_attn, mid_low, soft, cot, gains, router, dense, grads_out
    )
    grad_qkv = attend_back(pair_order, bounds, first_tile, qkv, grad_heads, kept)
    in_sum, dense_sum, grad_input, layer_out = last_sum(
        grad_qkv, proj, normed_low, attended, branch, grad_after, hidden, cosine, sine, gains,
        ffn_grad, router_grad, after_attn, outs, dense, grads_in,
    )
    total = dense_sum.astype(F32)
    return (
        layer_out[None],
        grad_input[None],
        total[32, 3072:3200],
        total[:, 0:1024],
        total[:, 1024:1536],
        total[:, 1536:2048],
        total[33, 3072:3200],
        total[34, 3072:3136],
        total[:, 2048:3072],
        total[35, 3072:3200],
        total[0:32, 3072:3200].T,
        in_sum[:, :, 0:FF],
        in_sum[:, :, FF:],
        out_sum,
    )


def solution(mesh):
    exp, tok = P("exp"), P("exp", "ctx", None)
    rows = P("exp", None)
    return jax.shard_map(
        body,
        mesh=mesh,
        in_specs=(
            tok, tok, rows, tok, tok, P(), exp, rows, rows, rows, exp, exp, rows, exp, rows,
            tok, tok, tok,
        ),
        out_specs=(
            tok, tok, exp, rows, rows, rows, exp, exp, rows, exp, rows, tok, tok, tok,
        ),
        check_vma=False,
    )
```

```python
import functools

import jax
import jax.numpy as jnp
from jax import lax
from jax.experimental import pallas as pl
from jax.experimental.pallas import tpu as pltpu
from jax.sharding import PartitionSpec as P

MESH = pl.DeviceIdType.MESH
BF = jnp.bfloat16
F32 = jnp.float32
HEADS = 16
KV_HEADS = 8
HEAD = 64
TOP = 8
EXP_DEV = 4
EXPERTS = 32
TOK = 192
HALF = 96
D = 1024
FF = 512
CAP = 48
SEQ = 3072
WIDE = D + 128
EPS = 1e-06
HIGH = lax.Precision.HIGHEST
MASKED = -1e30
VMEM_BYTES = 60 * 1024 * 1024


class Place:
    def __init__(self):
        self.c = lax.axis_index("ctx")
        self.e = lax.axis_index("exp")
        self.x, self.k = self.e // 2, self.e % 2
        self.y, self.z = self.c // 4, self.c % 4

    def exp_at(self, shift):
        return ((self.x + shift) % 4) * 2 + self.k

    def along_x(self, shift):
        return (self.c, self.exp_at(shift))

    def sibling(self):
        return (self.c, self.x * 2 + 1 - self.k)

    def ctx_at(self, half, first, second):
        if half == 0:
            return ((self.y + second) % 4) * 4 + (self.z + first) % 4
        return ((self.y + first) % 4) * 4 + (self.z + second) % 4

    def along_first(self, half, shift):
        return (self.ctx_at(half, shift, 0), self.e)

    def along_second(self, half, shift):
        return (self.ctx_at(half, 0, shift), self.e)

    def ctx_ahead(self, shift):
        return (self.c + shift) % 16


class Mail:
    def __init__(self, send_sems, recv_sems, place):
        self.send_sems, self.recv_sems, self.place = send_sems, recv_sems, place
        self.used, self.sent = 0, []

    def slots(self, number):
        first = self.used
        self.used += number
        return list(range(first, first + number))

    def send(self, slot, src, dst, device):
        copy = pltpu.make_async_remote_copy(
            src_ref=src,
            dst_ref=dst,
            send_sem=self.send_sems.at[slot],
            recv_sem=self.recv_sems.at[slot],
            device_id=device,
            device_id_type=MESH,
        )
        copy.start()
        self.sent.append(copy)

    def wait(self, slot, region):
        pltpu.make_async_remote_copy(
            src_ref=region,
            dst_ref=region,
            send_sem=self.send_sems.at[slot],
            recv_sem=self.recv_sems.at[slot],
            device_id=self.place.sibling(),
            device_id_type=MESH,
        ).wait_recv()

    def finish(self):
        for copy in self.sent:
            copy.wait_send()
        self.sent = []


def meet(devices):
    barrier = pltpu.get_barrier_semaphore()
    for device in devices:
        pl.semaphore_signal(barrier, inc=1, device_id=device, device_id_type=MESH)
    pl.semaphore_wait(barrier, len(devices))


def ring_x_peers(place):
    return [place.along_x(1), place.along_x(3), place.sibling()]


def ring_yz_peers(place):
    return [
        place.along_first(0, 1),
        place.along_first(0, 3),
        place.along_first(1, 1),
        place.along_first(1, 3),
    ]


def ctx_peers(place):
    return [(place.ctx_ahead(shift), place.e) for shift in range(1, 16)]


def pump(routines):
    for routine in routines:
        next(routine, None)


def drain(routine):
    for _ in routine:
        pass


def interleave(routines):
    routines = list(routines)
    while routines:
        for routine in list(routines):
            try:
                next(routine)
            except StopIteration:
                routines.remove(routine)


def gather_x(place, mail, out, rows):
    (to_right, to_left, to_sib, far0, far1, sib_l, sib_r, sib_f0, sib_f1) = mail.slots(9)
    half = rows // 2

    def shard(shift, core_same=True):
        exp = place.exp_at(shift) if core_same else place.exp_at(shift) + 1 - 2 * place.k
        if len(out.shape) == 3:
            return out.at[exp]
        return out.at[pl.ds(pl.multiple_of(exp * rows, 16), rows)]

    def part(shift, which, core_same=True):
        exp = place.exp_at(shift) if core_same else place.exp_at(shift) + 1 - 2 * place.k
        if len(out.shape) == 3:
            return out.at[exp, pl.ds(which * half, half)]
        return out.at[pl.ds(pl.multiple_of(exp * rows + which * half, 16), half)]

    right, left, sib = place.along_x(1), place.along_x(3), place.sibling()
    mail.send(to_right, shard(0), shard(0), right)
    mail.send(to_left, shard(0), shard(0), left)
    mail.send(to_sib, shard(0), shard(0), sib)
    yield
    mail.wait(to_right, shard(3))
    mail.send(far0, part(3, 0), part(3, 0), right)
    mail.send(sib_l, shard(3), shard(3), sib)
    mail.wait(to_left, shard(1))
    mail.send(far1, part(1, 1), part(1, 1), left)
    mail.send(sib_r, shard(1), shard(1), sib)
    yield
    mail.wait(far0, part(2, 0))
    mail.send(sib_f0, part(2, 0), part(2, 0), sib)
    mail.wait(far1, part(2, 1))
    mail.send(sib_f1, part(2, 1), part(2, 1), sib)
    yield
    mail.wait(to_sib, shard(0, False))
    mail.wait(sib_l, shard(3, False))
    mail.wait(sib_r, shard(1, False))
    mail.wait(sib_f0, part(2, 0, False))
    mail.wait(sib_f1, part(2, 1, False))


def gather_yz(place, mail, out, half, columns=slice(None)):
    first, second = (functools.partial(f, half) for f in (place.along_first, place.along_second))

    def piece(a, b):
        return out.at[pl.ds(2 * half, 2), place.ctx_at(half, a, b), :, columns]

    def quarter(a, b, which):
        return out.at[2 * half + which, place.ctx_at(half, a, b), :, columns]

    f_r, f_l, f_far0, f_far1 = mail.slots(4)
    mail.send(f_r, piece(0, 0), piece(0, 0), first(1))
    mail.send(f_l, piece(0, 0), piece(0, 0), first(3))
    s_slots = {a: mail.slots(2) for a in (0, 1, 3)}
    s_far = {a: mail.slots(2) for a in (0, 1, 2, 3)}
    s_quarters = mail.slots(4)
    mail.send(s_slots[0][0], piece(0, 0), piece(0, 0), second(1))
    mail.send(s_slots[0][1], piece(0, 0), piece(0, 0), second(3))
    yield
    mail.wait(f_r, piece(3, 0))
    mail.send(f_far0, quarter(3, 0, 0), quarter(3, 0, 0), first(1))
    mail.wait(f_l, piece(1, 0))
    mail.send(f_far1, quarter(1, 0, 1), quarter(1, 0, 1), first(3))
    for a in (3, 1):
        mail.send(s_slots[a][0], piece(a, 0), piece(a, 0), second(1))
        mail.send(s_slots[a][1], piece(a, 0), piece(a, 0), second(3))
    yield
    mail.wait(s_slots[0][0], piece(0, 3))
    mail.send(s_far[0][0], quarter(0, 3, 0), quarter(0, 3, 0), second(1))
    mail.wait(s_slots[0][1], piece(0, 1))
    mail.send(s_far[0][1], quarter(0, 1, 1), quarter(0, 1, 1), second(3))
    mail.wait(f_far0, quarter(2, 0, 0))
    mail.send(s_quarters[0], quarter(2, 0, 0), quarter(2, 0, 0), second(1))
    mail.send(s_quarters[1], quarter(2, 0, 0), quarter(2, 0, 0), second(3))
    mail.wait(f_far1, quarter(2, 0, 1))
    mail.send(s_quarters[2], quarter(2, 0, 1), quarter(2, 0, 1), second(1))
    mail.send(s_quarters[3], quarter(2, 0, 1), quarter(2, 0, 1), second(3))
    yield
    for a in (3, 1):
        mail.wait(s_slots[a][0], piece(a, 3))
        mail.send(s_far[a][0], quarter(a, 3, 0), quarter(a, 3, 0), second(1))
        mail.wait(s_slots[a][1], piece(a, 1))
        mail.send(s_far[a][1], quarter(a, 1, 1), quarter(a, 1, 1), second(3))
    yield
    mail.wait(s_quarters[0], quarter(2, 3, 0))
    mail.send(s_far[2][0], quarter(2, 3, 0), quarter(2, 3, 0), second(1))
    mail.wait(s_quarters[3], quarter(2, 1, 1))
    mail.send(s_far[2][1], quarter(2, 1, 1), quarter(2, 1, 1), second(3))
    mail.wait(s_quarters[1], quarter(2, 1, 0))
    mail.wait(s_quarters[2], quarter(2, 3, 1))
    yield
    for a in (0, 1, 2, 3):
        mail.wait(s_far[a][0], quarter(a, 2, 0))
        mail.wait(s_far[a][1], quarter(a, 2, 1))


GATHER_YZ_COPIES = 2 * 22


def add_rows(out, terms, rows, step=16):
    def body(i, _):
        at = pl.ds(pl.multiple_of(i * step, step), step)
        total = terms[0][at].astype(F32)
        for term in terms[1:]:
            total = total + term[at].astype(F32)
        out[at] = total.astype(out.dtype)
        return 0

    lax.fori_loop(0, rows // step, body, 0)


def scatter_x(place, mail, grads, out, sib_buf, sums, near, far, rows, extra=None):
    half = rows // 2
    s_sib = mail.slots(4)
    far0, far1, r_free, r_dep, l_free, l_dep = mail.slots(6)
    right, left, sib = place.along_x(1), place.along_x(3), place.sibling()
    for at, shift in enumerate((2, 1, 3, 0)):
        theirs = place.exp_at(shift) + 1 - 2 * place.k
        mail.send(s_sib[at], grads.at[theirs], sib_buf.at[at], sib)
    yield

    def mine(shift, which):
        return grads.at[place.exp_at(shift), pl.ds(which * half, half)]

    def from_sib(at, which):
        return sib_buf.at[at, pl.ds(which * half, half)]

    mail.wait(s_sib[0], sib_buf.at[0])
    add_rows(sums.at[0, 0], [mine(2, 0), from_sib(0, 0)], half)
    mail.send(far0, sums.at[0, 0], far.at[0], right)
    add_rows(sums.at[0, 1], [mine(2, 1), from_sib(0, 1)], half)
    mail.send(far1, sums.at[0, 1], far.at[1], left)
    yield
    mail.wait(s_sib[1], sib_buf.at[1])
    add_rows(sums.at[1, 1], [mine(1, 1), from_sib(1, 1)], half)
    mail.send(r_free, sums.at[1, 1], near.at[0, 1], right)
    mail.wait(s_sib[2], sib_buf.at[2])
    add_rows(sums.at[2, 0], [mine(3, 0), from_sib(2, 0)], half)
    mail.send(l_free, sums.at[2, 0], near.at[1, 0], left)
    yield
    mail.wait(far0, far.at[0])
    add_rows(sums.at[1, 0], [mine(1, 0), from_sib(1, 0), far.at[0]], half)
    mail.send(r_dep, sums.at[1, 0], near.at[0, 0], right)
    mail.wait(far1, far.at[1])
    add_rows(sums.at[2, 1], [mine(3, 1), from_sib(2, 1), far.at[1]], half)
    mail.send(l_dep, sums.at[2, 1], near.at[1, 1], left)
    yield
    mail.wait(s_sib[3], sib_buf.at[3])
    mail.wait(r_free, near.at[0, 1])
    mail.wait(l_free, near.at[1, 0])
    mail.wait(r_dep, near.at[0, 0])
    mail.wait(l_dep, near.at[1, 1])
    for which in (0, 1):
        at = pl.ds(which * half, half)
        terms = [mine(0, which), from_sib(3, which), near.at[0, which], near.at[1, which]]
        add_rows(out.at[at], terms + ([] if extra is None else [extra.at[at]]), half)


SCATTER_X_COPIES = 10


def scatter_x_scratch(rows, columns):
    half = rows // 2
    return [
        pltpu.VMEM((4, rows, columns), BF),
        pltpu.VMEM((3, 2, half, columns), BF),
        pltpu.VMEM((2, 2, half, columns), BF),
        pltpu.VMEM((2, half, columns), BF),
    ]


def scatter_yz(place, mail, grads, out, half, far, near, far2, near2):
    first, second = (functools.partial(f, half) for f in (place.along_first, place.along_second))
    rows = grads.shape[2]
    columns = slice(half * FF, half * FF + FF)

    def part(a, b, which):
        return grads.at[which, place.ctx_at(half, a, b), :, columns]

    order = (2, 1, 3, 0)
    sl_far = [mail.slots(2) for _ in order]
    sl_free = [mail.slots(2) for _ in order]
    sl_dep = [mail.slots(2) for _ in order]
    for at, a in enumerate(order):
        mail.send(sl_far[at][0], part(a, 2, 0), far.at[half, 0, at], second(1))
        mail.send(sl_far[at][1], part(a, 2, 1), far.at[half, 1, at], second(3))
    for at, a in enumerate(order):
        mail.send(sl_free[at][0], part(a, 1, 1), near.at[half, 0, 1, at], second(1))
        mail.send(sl_free[at][1], part(a, 3, 0), near.at[half, 1, 0, at], second(3))
    yield
    for at, a in enumerate(order):
        mail.wait(sl_far[at][0], far.at[half, 0, at])
        add_rows(part(a, 1, 0), [part(a, 1, 0), far.at[half, 0, at]], rows)
        mail.send(sl_dep[at][0], part(a, 1, 0), near.at[half, 0, 0, at], second(1))
        mail.wait(sl_far[at][1], far.at[half, 1, at])
        add_rows(part(a, 3, 1), [part(a, 3, 1), far.at[half, 1, at]], rows)
        mail.send(sl_dep[at][1], part(a, 3, 1), near.at[half, 1, 1, at], second(3))
    yield
    m_far, m_free, m_dep = mail.slots(2), mail.slots(2), mail.slots(2)
    for at, a in enumerate(order):
        mail.wait(sl_free[at][0], near.at[half, 0, 1, at])
        mail.wait(sl_free[at][1], near.at[half, 1, 0, at])
        mail.wait(sl_dep[at][0], near.at[half, 0, 0, at])
        mail.wait(sl_dep[at][1], near.at[half, 1, 1, at])
        for which in (0, 1):
            own = part(a, 0, which)
            add_rows(own, [own, near.at[half, 0, which, at], near.at[half, 1, which, at]], rows)
        if a == 2:
            mail.send(m_far[0], part(2, 0, 0), far2.at[half, 0], first(1))
            mail.send(m_far[1], part(2, 0, 1), far2.at[half, 1], first(3))
        if a == 1:
            mail.send(m_free[0], part(1, 0, 1), near2.at[half, 0, 1], first(1))
        if a == 3:
            mail.send(m_free[1], part(3, 0, 0), near2.at[half, 1, 0], first(3))
    yield
    mail.wait(m_far[0], far2.at[half, 0])
    add_rows(part(1, 0, 0), [part(1, 0, 0), far2.at[half, 0]], rows)
    mail.send(m_dep[0], part(1, 0, 0), near2.at[half, 0, 0], first(1))
    mail.wait(m_far[1], far2.at[half, 1])
    add_rows(part(3, 0, 1), [part(3, 0, 1), far2.at[half, 1]], rows)
    mail.send(m_dep[1], part(3, 0, 1), near2.at[half, 1, 1], first(3))
    yield
    mail.wait(m_free[0], near2.at[half, 0, 1])
    mail.wait(m_free[1], near2.at[half, 1, 0])
    mail.wait(m_dep[0], near2.at[half, 0, 0])
    mail.wait(m_dep[1], near2.at[half, 1, 1])
    for which in (0, 1):
        add_rows(
            out.at[which, :, columns],
            [part(0, 0, which), near2.at[half, 0, which], near2.at[half, 1, which]],
            rows,
        )


SCATTER_YZ_COPIES = 2 * 30


def scatter_yz_scratch():
    one = (96, FF)
    return [
        pltpu.VMEM((2, 2, 4) + one, BF),
        pltpu.VMEM((2, 2, 2, 4) + one, BF),
        pltpu.VMEM((2, 2) + one, BF),
        pltpu.VMEM((2, 2, 2) + one, BF),
    ]


SUM_ROWS = 16


def sum_ctx(place, mail, mine, out, slots):
    up, down = mail.slots(15), mail.slots(15)
    half = mine.shape[1] // 2

    def piece(ref, c):
        return ref.at[
            pl.ds(pl.multiple_of((c // 2) * SUM_ROWS, SUM_ROWS), SUM_ROWS),
            pl.ds(pl.multiple_of((c % 2) * half, 128), half),
        ]

    for shift in range(1, 16):
        c = place.ctx_ahead(shift)
        mail.send(up[shift - 1], piece(mine, c), slots.at[shift], (c, place.e))
    yield
    for shift in range(1, 16):
        mail.wait(up[shift - 1], slots.at[shift])
    total = piece(mine, place.c)[...].astype(F32)
    for shift in range(1, 16):
        total = total + slots[shift].astype(F32)
    own = piece(out, place.c)
    own[...] = total.astype(BF)
    for shift in range(1, 16):
        c = place.ctx_ahead(shift)
        mail.send(down[shift - 1], own, own, (c, place.e))
    yield
    for shift in range(1, 16):
        mail.wait(down[shift - 1], piece(out, place.ctx_ahead(16 - shift)))


def any_spec():
    return pl.BlockSpec(memory_space=pl.ANY)


def vmem_spec():
    return pl.BlockSpec(memory_space=pltpu.VMEM)


def sends(body, number, outs, args, in_specs, out_specs, scratch, collective_id):
    return pl.pallas_call(
        body,
        out_shape=outs,
        in_specs=in_specs,
        out_specs=out_specs,
        scratch_shapes=list(scratch)
        + [pltpu.SemaphoreType.DMA((number,)), pltpu.SemaphoreType.DMA((number,))],
        compiler_params=pltpu.CompilerParams(
            collective_id=collective_id, has_side_effects=True, vmem_limit_bytes=VMEM_BYTES
        ),
    )(*args)


def pack_pair(sent, kind, heads, low, high):
    one, two = swap_pair(low, high)
    for head in heads[0]:
        sent[head, kind] = one.astype(BF)
    for head in heads[1]:
        sent[head, kind] = two.astype(BF)


def swap_heads(place, mail, sent, arrived):
    slots = mail.slots(15)
    for shift in range(1, 16):
        c = place.ctx_ahead(shift)
        mail.send(slots[shift - 1], sent.at[c], arrived.at[place.c], (c, place.e))
    arrived[place.c] = sent[place.c]
    yield
    for shift in range(1, 16):
        mail.wait(slots[shift - 1], arrived.at[place.ctx_ahead(16 - shift)])


def slot_matrix(routes, order_row, order_column):
    wide = TOP * EXPERTS
    lane = lane_of((TOK, wide))
    named = jnp.zeros((TOK, wide), jnp.int32)
    for m in range(TOP):
        named = jnp.where(lane // EXPERTS == m, routes[:, m : m + 1], named)
    hit = jnp.where(named == lane % EXPERTS, 1.0, 0.0)
    before = jnp.where(order_row < order_column, 1.0, 0.0).astype(BF)
    inside = jnp.dot(before, hit.astype(BF), preferred_element_type=F32)
    counts = jnp.broadcast_to(jnp.sum(hit, axis=0, keepdims=True), (16, wide)).astype(BF)
    src = lax.broadcasted_iota(jnp.int32, (wide, wide), 0)
    dst = lax.broadcasted_iota(jnp.int32, (wide, wide), 1)
    earlier_of = (src % EXPERTS == dst % EXPERTS) & (src // EXPERTS < dst // EXPERTS)
    earlier = jnp.dot(counts, jnp.where(earlier_of, 1.0, 0.0).astype(BF), preferred_element_type=F32)
    slot = hit * jnp.minimum(inside + earlier[0:1], 64.0)
    src = lax.broadcasted_iota(jnp.int32, (wide, 128), 0)
    dst = lax.broadcasted_iota(jnp.int32, (wide, 128), 1)
    fold = jnp.where((src % EXPERTS == dst % EXPERTS) & (dst < 2 * EXPERTS), 1.0, 0.0).astype(BF)
    slot = jnp.dot(slot.astype(BF), fold, preferred_element_type=F32)
    named = jnp.dot(hit.astype(BF), fold, preferred_element_type=F32)
    return jnp.where((named > 0.5) & (slot < CAP - 0.5), slot, -1.0)


def pair_angles(first_block, freqs):
    row = lax.broadcasted_iota(jnp.int32, (TOK, 128), 0)
    lane = lane_of((TOK, 128))
    at = jnp.where(row < HALF, first_block * HALF + row, (31 - first_block) * HALF + row - HALF)
    turned = at.astype(F32) * freqs
    sine = jnp.sin(turned)
    return jnp.cos(turned), jnp.where(lane % HEAD < HEAD // 2, -sine, sine)


def pack_pair(sent, kind, heads, low, high):
    one, two = swap_pair(low, high)
    for head in heads[0]:
        sent[head, kind] = one.astype(BF)
    for head in heads[1]:
        sent[head, kind] = two.astype(BF)


def swap_heads(place, mail, sent, arrived):
    slots = mail.slots(15)
    for shift in range(1, 16):
        c = place.ctx_ahead(shift)
        mail.send(slots[shift - 1], sent.at[c], arrived.at[place.c], (c, place.e))
    arrived[place.c] = sent[place.c]
    yield
    for shift in range(1, 16):
        mail.wait(slots[shift - 1], arrived.at[place.ctx_ahead(16 - shift)])


def attend_tiles(bounds, inverse, order, qkv, kept, sent, qs, ks, vs, vt, outs):
    for spot in range(16):
        c = inverse[spot]
        low = slice(spot * HALF, spot * HALF + HALF)
        high = slice((31 - spot) * HALF, (31 - spot) * HALF + HALF)
        for kind, dst, scale in ((0, qs, 0.125), (1, ks, 1.0), (2, vs, 1.0)):
            block = qkv[c, kind] * scale
            dst[low, :] = block[:, 0:HEAD]
            dst[high, :] = block[:, HEAD : 2 * HEAD]
    for i in range(SEQ // 256):
        at = slice(i * 256, i * 256 + 256)
        vt[:, at] = vs[at, :].astype(F32).T.astype(BF)
    yield
    for i in range(SEQ // ATT):
        at = slice(i * ATT, i * ATT + ATT)
        query = qs[at, :]
        query_at = lax.broadcasted_iota(jnp.int32, (1, ATT), 1) + i * ATT
        start = jnp.zeros((1, ATT), jnp.int32)
        for d in range(3):
            start = jnp.where(query_at >= bounds[d], bounds[d], start)

        def step(j, state, last, query=query, query_at=query_at, start=start):
            peak, total, acc = state
            here = pl.ds(pl.multiple_of(j * ATT, ATT), ATT)
            scores = dot_tt(ks[here, :], query, ((1,), (1,)))
            key_at = lax.broadcasted_iota(jnp.int32, (ATT, ATT), 0)
            known = key_at >= start - j * ATT
            if last:
                known = known & (key_at <= query_at - j * ATT)
            scores = jnp.where(known, scores, MASKED)
            new_peak = jnp.maximum(peak, jnp.max(scores, axis=0, keepdims=True))
            weights = jnp.exp(scores - new_peak)
            keep = jnp.exp(peak - new_peak)
            total = total * keep + jnp.sum(weights, axis=0, keepdims=True)
            acc = acc * keep + dot_tt(vt[:, here], weights.astype(BF), ((1,), (0,)))
            return new_peak, total, acc

        state = (
            jnp.full((1, ATT), MASKED, F32),
            jnp.zeros((1, ATT), F32),
            jnp.zeros((HEAD, ATT), F32),
        )
        if i > 0:
            state = lax.fori_loop(0, i, functools.partial(step, last=False), state)
        peak, total, acc = step(i, state, True)
        mixed = acc / total
        kept[0:HEAD, at] = mixed
        kept[HEAD : HEAD + 8, at] = jnp.broadcast_to(peak + jnp.log(total), (8, ATT))
        blocks = ATT // HALF
        outs[i * blocks : i * blocks + blocks] = mixed.T.reshape(blocks, HALF, HEAD)
        yield
    for c in range(16):
        spot = order[c]
        sent[c, 0] = jnp.concatenate([outs[spot], outs[31 - spot]], axis=1).astype(BF)


def front_body(
    order, inverse, bounds,
    w_query, w_key, w_value, w_output, misc, cot, routes, order_row, order_column,
    w_gate, w_up, w_down, hidden, freqs,
    dense_out, w_out_all, cots, w_in, w_out, tokens,
    qkv, kept, proj, normed_low, gains, router, cosine, sine, attended, after, mid_low, soft,
    dense, weight, slots_own, sent, heads, arrived, mine, qs, ks, vs, vt, outs,
    local_sems, send_sems, recv_sems,
):
    place = Place()
    mail = Mail(send_sems, recv_sems, place)
    row = pl.ds(pl.multiple_of(place.e * 128, 128), 128)
    copies = [
        pltpu.make_async_copy(src, dst, local_sems.at[i])
        for i, (src, dst) in enumerate(
            [
                (w_gate, w_in.at[:, place.c, :, pl.ds(0, FF)]),
                (w_up, w_in.at[:, place.c, :, pl.ds(FF, FF)]),
                (w_down, w_out.at[:, place.c]),
                (cot, cots.at[place.e, :, pl.ds(0, D)]),
            ]
        )
    ]
    for copy in copies:
        copy.start()
    dense[row, 0:1024] = w_query[...]
    dense[row, 1024:1536] = w_key[...]
    dense[row, 1536:2048] = w_value[...]
    dense[row, 2048:FRONT] = misc[...]
    weight[row, :] = w_output[...]
    for copy in copies:
        copy.wait()
    meet(ring_x_peers(place) + ctx_peers(place))

    gate = [gather_yz(place, mail, w_in, h, slice(0, FF)) for h in (0, 1)]
    up = [gather_yz(place, mail, w_in, h, slice(FF, 2 * FF)) for h in (0, 1)]
    down = [gather_yz(place, mail, w_out, h) for h in (0, 1)]
    qkv_weight = gather_x(place, mail, dense, 128)
    output_weight = gather_x(place, mail, weight, 128)
    cot_rows = gather_x(place, mail, cots, TOK)

    pump([qkv_weight] + gate)
    table = slot_matrix(routes[...], order_row[...], order_column[...])
    slots_own[...] = table.astype(BF)
    place_slots = pltpu.make_async_copy(
        slots_own, cots.at[place.e, :, pl.ds(D, 128)], local_sems.at[4]
    )
    place_slots.start()
    cosine[...], sine[...] = pair_angles(order[place.c], freqs[...])
    scale = rms_rows(hidden[...].astype(F32))
    place_slots.wait()
    pump(gate + [qkv_weight])
    pump(gate + [qkv_weight])
    pump([output_weight, cot_rows])
    pump(gate)
    drain(qkv_weight)
    keep = pltpu.make_async_copy(dense.at[:, pl.ds(0, 2048)], dense_out, local_sems.at[5])
    keep.start()
    pump(gate)

    def project():
        router[...] = jnp.zeros_like(router)
        gains[...] = jnp.zeros_like(gains)
        for e in range(8):
            at = slice(e * 128, e * 128 + 128)
            block = dense[e * 128 : e * 128 + 48, 2048:2176].astype(F32)
            router[0:32, at] = block[0:32].astype(BF)
            router[32:64, at] = block[0:32].astype(BF)
            gains[0:2, at] = block[32:34]
            gains[2:3, e * 64 : e * 64 + 64] = block[34:35, 0:64]
            gains[3:4, at] = block[35:36]
        normed_low[...] = (hidden[...].astype(F32) * scale * gains[0:1, :]).astype(BF)
        for n in range(4):
            at = slice(n * 512, n * 512 + 512)
            proj[:, at] = jnp.dot(normed_low[...], dense[:, at], preferred_element_type=F32)
        query_scale = rms_rows(proj[:, 0:1024])
        key_scale = rms_rows(proj[:, 1024:1536])
        low, high = slice(0, HALF), slice(HALF, TOK)
        for g in range(8):
            at = slice(g * 128, g * 128 + 128)
            values = proj[:, at] * query_scale * gains[1:2, at]
            pack_pair(
                sent, 0, ((2 * g,), (2 * g + 1,)),
                turn_pair(values[low], cosine[low, :], sine[low, :]),
                turn_pair(values[high], cosine[high, :], sine[high, :]),
            )
        for g in range(4):
            at = slice(1024 + g * 128, 1024 + g * 128 + 128)
            pair = ((4 * g, 4 * g + 1), (4 * g + 2, 4 * g + 3))
            values = proj[:, at] * key_scale * gains[2:3, g * 128 : g * 128 + 128]
            pack_pair(
                sent, 1, pair,
                turn_pair(values[low], cosine[low, :], sine[low, :]),
                turn_pair(values[high], cosine[high, :], sine[high, :]),
            )
            at = slice(1536 + g * 128, 1536 + g * 128 + 128)
            pack_pair(sent, 2, pair, proj[low, at], proj[high, at])

    project()
    swap = swap_heads(place, mail, sent, qkv)
    pump([swap] + gate)
    pump([output_weight, cot_rows] + gate)
    drain(swap)
    pump(up)
    tiles = attend_tiles(bounds, inverse, order, qkv, kept, heads, qs, ks, vs, vt, outs)
    pump([tiles, output_weight, cot_rows])
    pump([tiles])
    pump([tiles])
    pump([tiles, output_weight, cot_rows])
    keep.wait()
    keep_weight = pltpu.make_async_copy(weight, w_out_all, local_sems.at[6])
    pump([tiles])
    pump([tiles])
    pump([tiles] + up)
    pump([tiles])
    drain(tiles)
    swap = swap_heads(place, mail, heads, arrived)
    pump([swap] + up)
    drain(output_weight)
    keep_weight.start()
    drain(cot_rows)
    pump(up)
    drain(swap)

    def middle():
        for g in range(8):
            at = slice(g * 128, g * 128 + 128)
            pair = swap_pair(arrived[2 * g, 0].astype(F32), arrived[2 * g + 1, 0].astype(F32))
            attended[0:HALF, at] = pair[0].astype(BF)
            attended[HALF:TOK, at] = pair[1].astype(BF)
        values = hidden[...].astype(F32) + jnp.dot(
            attended[...], weight[...], preferred_element_type=F32
        )
        after[...] = values
        mid_low[...] = (values * rms_rows(values) * gains[3:4, :]).astype(BF)
        logits = dot_tt(mid_low[...], router[...], ((1,), (1,)))
        lane = lane_of((TOK, 128))
        known = lane < EXPERTS
        peak = jnp.max(jnp.where(known, logits, MASKED), axis=1, keepdims=True)
        weights = jnp.exp(jnp.where(lane < 2 * EXPERTS, logits, MASKED) - peak)
        probs = weights / jnp.sum(jnp.where(known, weights, 0.0), axis=1, keepdims=True)
        soft[...] = probs
        gates = jnp.where(slots_own[...].astype(F32) >= 0, probs, 0.0)
        gates_high = gates.astype(BF).astype(F32)
        mine[:, 0:D] = mid_low[...]
        mine[:, D:WIDE] = jnp.where(known, gates_high, gates - gates_high).astype(BF)
        place_rows = pltpu.make_async_copy(mine, tokens.at[place.e], local_sems.at[7])
        place_rows.start()
        place_rows.wait()

    middle()
    token_rows = gather_x(place, mail, tokens, TOK)
    pump([token_rows] + up + down)
    pump(up + down)
    pump(down + [token_rows])
    pump(down + [token_rows])
    pump(down)
    drain(token_rows)
    for routine in gate + up + down:
        drain(routine)
    keep_weight.wait()
    mail.finish()


FRONT = 2304
ATT = 384


def front(*args):
    return sends(
        front_body,
        3 * GATHER_YZ_COPIES + 36 + 30,
        [
            jax.ShapeDtypeStruct((1024, 2048), BF),
            jax.ShapeDtypeStruct((1024, 1024), BF),
            jax.ShapeDtypeStruct((8, TOK, WIDE), BF),
            jax.ShapeDtypeStruct((4, 16, 64, 1024), BF),
            jax.ShapeDtypeStruct((4, 16, 32, 1024), BF),
            jax.ShapeDtypeStruct((8, TOK, WIDE), BF),
            jax.ShapeDtypeStruct((16, 3, HALF, 128), BF),
            jax.ShapeDtypeStruct((HEAD + 8, SEQ), F32),
            jax.ShapeDtypeStruct((TOK, 2048), F32),
            jax.ShapeDtypeStruct((TOK, D), BF),
            jax.ShapeDtypeStruct((8, D), F32),
            jax.ShapeDtypeStruct((128, D), BF),
            jax.ShapeDtypeStruct((TOK, 128), F32),
            jax.ShapeDtypeStruct((TOK, 128), F32),
            jax.ShapeDtypeStruct((TOK, D), BF),
            jax.ShapeDtypeStruct((TOK, D), F32),
            jax.ShapeDtypeStruct((TOK, D), BF),
            jax.ShapeDtypeStruct((TOK, 128), F32),
        ],
        args,
        [smem_spec()] * 3 + [vmem_spec()] * 14,
        [any_spec()] * 6 + [vmem_spec()] * 12,
        [
            pltpu.VMEM((1024, FRONT), BF),
            pltpu.VMEM((1024, 1024), BF),
            pltpu.VMEM((TOK, 128), BF),
            pltpu.VMEM((16, 3, HALF, 128), BF),
            pltpu.VMEM((16, 1, HALF, 128), BF),
            pltpu.VMEM((16, 1, HALF, 128), BF),
            pltpu.VMEM((TOK, WIDE), BF),
        ]
        + [pltpu.VMEM((SEQ, HEAD), BF)] * 3
        + [
            pltpu.VMEM((HEAD, SEQ), BF),
            pltpu.VMEM((SEQ // HALF, HALF, HEAD), F32),
            pltpu.SemaphoreType.DMA((8,)),
        ],
        1,
    )


def pick_rows(place, tok, cot, pick, rows_in, rows_cot, gate_rows):
    lane = lane_of((1, 128))

    def source(s, _):
        slots_t = cot[s, :, D:WIDE].astype(F32).T
        slot_at = lax.broadcasted_iota(jnp.int32, (CAP, TOK), 0).astype(F32)
        rows_at = lax.broadcasted_iota(jnp.int32, (128, TOK), 0)
        parts = []
        for n in range(EXP_DEV):
            line = jnp.sum(
                jnp.where(rows_at == place.e * EXP_DEV + n, slots_t, 0.0), axis=0, keepdims=True
            )
            parts.append(jnp.where(slot_at == line, 1.0, 0.0))
        chosen = jnp.concatenate(parts, axis=0).astype(BF)
        pick[s] = chosen
        moved = jnp.dot(chosen, tok[s], preferred_element_type=F32)
        turned = jnp.dot(chosen, cot[s, :, 0:D], preferred_element_type=F32)
        here = pl.ds(pl.multiple_of(s * CAP, 16), CAP)
        for n in range(EXP_DEV):
            part = slice(n * CAP, (n + 1) * CAP)
            rows_in[n, here, :] = moved[part, 0:D].astype(BF)
            rows_cot[n, here, :] = turned[part].astype(BF)
            wanted = place.e * EXP_DEV + n
            gate = jnp.sum(
                jnp.where((lane == wanted) | (lane == wanted + EXPERTS), moved[part, D:WIDE], 0.0),
                axis=1,
                keepdims=True,
            )
            gate_rows[n, here, :] = jnp.broadcast_to(gate, (CAP, 128))
        return 0

    lax.fori_loop(0, 8, source, 0)


def one_expert(place, j, w_in, w_out, grads, rows_in, rows_cot, gate_rows, spread):
    lane = lane_of((1, 128))
    weight_in = w_in[...].reshape(D, 2 * FF)
    weight_out = w_out[...].reshape(FF, D)
    x = rows_in[j]
    gate = gate_rows[j][:, 0:1]
    acts = jnp.dot(x, weight_in, preferred_element_type=F32)
    gate_act, up_act = acts[:, 0:FF], acts[:, FF:]
    sig = 1.0 / (1.0 + jnp.exp(-gate_act))
    silu = gate_act * sig
    inner = (silu * up_act).astype(BF)
    result = jnp.dot(inner, weight_out, preferred_element_type=F32)
    cot = rows_cot[j].astype(F32)
    grad_gate = jnp.sum(cot * result, axis=1, keepdims=True)
    grad_rows = (gate * cot).astype(BF)
    grad_inner = dot_tt(grad_rows, weight_out, ((1,), (1,)))
    grad_acts = jnp.concatenate(
        [grad_inner * up_act * (sig * (1.0 + gate_act * (1.0 - sig))), grad_inner * silu], axis=1
    ).astype(BF)
    for n in range(2):
        at = slice(n * 256, n * 256 + 256)
        grads[n * 8 : n * 8 + 8, 64:96, :] = (
            dot_tt(inner[:, at], grad_rows, ((0,), (0,))).astype(BF).reshape(8, 32, D)
        )
    for n in range(4):
        at = slice(n * 256, n * 256 + 256)
        grads[n * 4 : n * 4 + 4, 0:64, :] = (
            dot_tt(x[:, at], grad_acts, ((0,), (0,))).astype(BF).reshape(4, 64, D)
        )
    grad_high = grad_gate.astype(BF).astype(F32)
    wanted = place.e * EXP_DEV + j
    spread[j] = jnp.where(
        lane == wanted,
        grad_high,
        jnp.where(lane == wanted + EXPERTS, grad_gate - grad_high, 0.0),
    ).astype(BF)
    rows_in[j] = (gate * result).astype(BF)
    rows_cot[j] = dot_tt(grad_acts, weight_in, ((1,), (1,))).astype(BF)


def core_body(
    after, mid_low, soft, cot, gains, router, weight_hbm, tokens, cots, w_in, w_out,
    grad_after, branch, ffn_grad, router_grad, grad_heads, pair_sum, outs, late_grads,
    *rest,
):
    x, yz = rest[0:4], rest[4:8]
    (mid, weight, sent, tok, cot_rows, buf_in, buf_out, pick, rows_in, rows_cot, gate_rows, spread,
     early, late, local_sems, send_sems, recv_sems) = rest[8:]
    place = Place()
    mail = Mail(send_sems, recv_sems, place)
    loads = [
        pltpu.make_async_copy(src, dst, local_sems.at[i])
        for i, (src, dst) in enumerate([(tokens, tok), (cots, cot_rows), (weight_hbm, weight)])
    ]
    for load in loads:
        load.start()

    def fetch(j):
        copies = [
            pltpu.make_async_copy(w_in.at[j], buf_in.at[j % 2], local_sems.at[3 + 2 * (j % 2)]),
            pltpu.make_async_copy(w_out.at[j], buf_out.at[j % 2], local_sems.at[4 + 2 * (j % 2)]),
        ]
        for copy in copies:
            copy.start()
        return copies

    fetched = [fetch(0), fetch(1)]
    meet(ring_x_peers(place) + ctx_peers(place))
    loads[0].wait()
    loads[1].wait()
    pick_rows(place, tok, cot_rows, pick, rows_in, rows_cot, gate_rows)
    pair = [scatter_yz(place, mail, early, pair_sum, h, *yz) for h in (0, 1)]
    keep = None
    for j in range(EXP_DEV):
        for copy in fetched[j]:
            copy.wait()
        target = early.at[j] if j < 2 else late.at[j - 2]
        one_expert(
            place, j, buf_in.at[j % 2], buf_out.at[j % 2], target, rows_in, rows_cot, gate_rows, spread
        )
        if j + 2 < EXP_DEV:
            fetched.append(fetch(j + 2))
        if j == 1:
            pump(pair)
        if j == 3:
            keep = pltpu.make_async_copy(late, late_grads, local_sems.at[7])
            keep.start()

    def combine(s, _):
        here = pl.ds(pl.multiple_of(s * CAP, 16), CAP)
        chosen = pick[s]
        back = jnp.concatenate([rows_cot[n, here, :] for n in range(EXP_DEV)], axis=0)
        tok[s, :, 0:D] = dot_tt(chosen, back, ((0,), (0,))).astype(BF)
        back = jnp.concatenate([spread[n, here, :] for n in range(EXP_DEV)], axis=0)
        tok[s, :, D:WIDE] = dot_tt(chosen, back, ((0,), (0,))).astype(BF)
        back = jnp.concatenate([rows_in[n, here, :] for n in range(EXP_DEV)], axis=0)
        cot_rows[s, :, 0:D] = dot_tt(chosen, back, ((0,), (0,))).astype(BF)
        return 0

    lax.fori_loop(0, 8, combine, 0)
    mids = scatter_x(place, mail, tok, mid, *x, TOK)
    pump([mids])
    keep_outs = pltpu.make_async_copy(cot_rows.at[:, :, pl.ds(0, D)], outs, local_sems.at[8])
    keep_outs.start()
    pump([mids] + pair)
    drain(mids)

    def middle_back():
        lane = lane_of((TOK, 128))
        known = lane < EXPERTS
        halves = mid[:, D:WIDE]
        gate_grads = jnp.where(known, halves + pltpu.roll(halves, 96, 1), 0.0)
        probs = jnp.where(known, soft[...], 0.0)
        grad_logits = probs * (
            gate_grads - jnp.sum(probs * gate_grads, axis=1, keepdims=True)
        )
        high = grad_logits.astype(BF).astype(F32)
        split = (high + pltpu.roll(grad_logits - high, EXPERTS, 1)).astype(BF)
        grad_mid = mid[:, 0:D] + jnp.dot(split, router[...], preferred_element_type=F32)
        both = dot_tt(split, mid_low[...], ((0,), (0,)))
        router_grad[...] = both[0:EXPERTS] + both[EXPERTS : 2 * EXPERTS]
        values = after[...]
        back, gain_grad = norm_back(values, gains[3:4, :], grad_mid, rms_rows(values))
        ffn_grad[...] = gain_grad
        total = cot[...].astype(F32) + back
        grad_after[...] = total
        branch[...] = total.astype(BF)
        loads[2].wait()
        grad_attended = dot_tt(branch[...], weight[...], ((1,), (1,)))
        for g in range(8):
            at = slice(g * 128, g * 128 + 128)
            pack_pair(
                sent, 0, ((2 * g,), (2 * g + 1,)), grad_attended[0:HALF, at], grad_attended[HALF:TOK, at]
            )

    middle_back()
    swap = swap_heads(place, mail, sent, grad_heads)
    pump([swap] + pair)
    pump(pair)
    drain(swap)
    for routine in pair:
        drain(routine)
    keep.wait()
    keep_outs.wait()
    mail.finish()


def core(*args):
    return sends(
        core_body,
        SCATTER_YZ_COPIES + SCATTER_X_COPIES + 15,
        [
            jax.ShapeDtypeStruct((TOK, D), F32),
            jax.ShapeDtypeStruct((TOK, D), BF),
            jax.ShapeDtypeStruct((1, D), F32),
            jax.ShapeDtypeStruct((EXPERTS, D), F32),
            jax.ShapeDtypeStruct((16, 1, HALF, 128), BF),
            jax.ShapeDtypeStruct((2, 96, 1024), F32),
            jax.ShapeDtypeStruct((8, TOK, D), BF),
            jax.ShapeDtypeStruct((2, 16, 96, 1024), BF),
        ],
        args,
        [vmem_spec()] * 6 + [any_spec()] * 5,
        [vmem_spec()] * 6 + [any_spec()] * 2,
        scatter_x_scratch(TOK, WIDE)
        + scatter_yz_scratch()
        + [
            pltpu.VMEM((TOK, WIDE), F32),
            pltpu.VMEM((D, D), BF),
            pltpu.VMEM((16, 1, HALF, 128), BF),
            pltpu.VMEM((8, TOK, WIDE), BF),
            pltpu.VMEM((8, TOK, WIDE), BF),
            pltpu.VMEM((2, 16, 64, 1024), BF),
            pltpu.VMEM((2, 16, 32, 1024), BF),
            pltpu.VMEM((8, TOK, TOK), BF),
            pltpu.VMEM((EXP_DEV, 8 * CAP, D), BF),
            pltpu.VMEM((EXP_DEV, 8 * CAP, D), BF),
            pltpu.VMEM((EXP_DEV, 8 * CAP, 128), F32),
            pltpu.VMEM((EXP_DEV, 8 * CAP, 128), BF),
            pltpu.VMEM((2, 16, 96, 1024), BF),
            pltpu.VMEM((2, 16, 96, 1024), BF),
            pltpu.SemaphoreType.DMA((9,)),
        ],
        3,
    )


def dot_tt(a, b, dims):
    return lax.dot_general(a, b, (dims, ((), ())), preferred_element_type=F32)


def lane_of(shape):
    return lax.broadcasted_iota(jnp.int32, shape, len(shape) - 1)


def turn_pair(values, cosine, sine):
    first = lane_of(values.shape) % HEAD < HEAD // 2
    other = jnp.where(first, pltpu.roll(values, 96, 1), pltpu.roll(values, 32, 1))
    return values * cosine + other * sine


def swap_pair(one, two):
    low = lane_of(one.shape) < HEAD
    return (
        jnp.where(low, one, pltpu.roll(two, HEAD, 1)),
        jnp.where(low, pltpu.roll(one, HEAD, 1), two),
    )


def norm_back(values, gain, grad, scale_rows):
    inner = jnp.mean(values * gain * grad, axis=1, keepdims=True)
    back = scale_rows * gain * grad - values * (scale_rows * scale_rows * scale_rows * inner)
    return back, jnp.sum(grad * values * scale_rows, axis=0, keepdims=True)


def rms_rows(values):
    return lax.rsqrt(jnp.mean(values * values, axis=1, keepdims=True) + EPS)


def last_body(
    heads, proj, normed_low, attended, branch, after, hidden, cosine, sine, gains, ffn_grad, router_grad,
    after_attn, outs, dense, late_grads,
    pair_sum, query_sum, rest_sum, output_sum, grad_input, layer_out,
    *rest,
):
    yz, x_outs, query_x, rest_x, output_x = rest[0:4], rest[4:8], rest[8:12], rest[12:16], rest[16:20]
    query_mine, query_slots, query_grads, rest_mine, rest_slots, rest_grads = rest[20:26]
    output_mine, output_slots, output_grads = rest[26:29]
    late, weight, local_sems, arrived, turned, grad_proj, gain_rows, send_sems, recv_sems = rest[29:]
    place = Place()
    mail = Mail(send_sems, recv_sems, place)
    load = pltpu.make_async_copy(dense, weight, local_sems.at[0])
    load.start()
    load_late = pltpu.make_async_copy(late_grads, late, local_sems.at[1])
    load_late.start()
    meet(ring_x_peers(place) + ctx_peers(place))

    def unpack():
        for g in range(8):
            at = slice(g * 128, g * 128 + 128)
            parts = swap_pair(arrived[2 * g, 0].astype(F32), arrived[2 * g + 1, 0].astype(F32))
            for which in (0, 1):
                rows = slice(which * HALF, which * HALF + HALF)
                turned[rows, at] = turn_pair(parts[which], cosine[rows, :], -sine[rows, :])
        for g in range(4):
            for kind in (1, 2):
                parts = swap_pair(
                    arrived[4 * g, kind].astype(F32) + arrived[4 * g + 1, kind].astype(F32),
                    arrived[4 * g + 2, kind].astype(F32) + arrived[4 * g + 3, kind].astype(F32),
                )
                for which in (0, 1):
                    rows = slice(which * HALF, which * HALF + HALF)
                    if kind == 1:
                        turned[rows, 1024 + g * 128 : 1152 + g * 128] = turn_pair(
                            parts[which], cosine[rows, :], -sine[rows, :]
                        )
                    else:
                        grad_proj[rows, 1536 + g * 128 : 1664 + g * 128] = parts[which].astype(BF)

    def norms_back():
        gain_rows[...] = jnp.zeros_like(gain_rows)
        gain_rows[3:4, :] = ffn_grad[...]
        for n, (start, width) in enumerate(((0, 1024), (1024, 512))):
            at = slice(start, start + width)
            values = proj[:, at]
            back, gain_grad = norm_back(
                values, gains[1 + n : 2 + n, 0:width], turned[:, at], rms_rows(values)
            )
            grad_proj[:, at] = back.astype(BF)
            if n == 0:
                gain_rows[1:2, :] = gain_grad
            else:
                for e in range(8):
                    gain_rows[2:3, e * 128 : e * 128 + 64] = gain_grad[:, e * 64 : e * 64 + 64]

    def input_back():
        load.wait()
        grad_normed = dot_tt(grad_proj[...], weight[...], ((1,), (1,)))
        values = hidden[...].astype(F32)
        back, gain_grad = norm_back(values, gains[0:1, :], grad_normed, rms_rows(values))
        grad_input[...] = after[...] + back
        gain_rows[0:1, :] = gain_grad

    def weight_grads(rows, grads):
        return dot_tt(rows[...], grads, ((0,), (0,))).astype(BF).reshape(8, 128, grads.shape[1])

    def small_grads():
        rest_grads[:, :, 1024:REST] = jnp.zeros((8, 128, REST - 1024), BF)
        for e in range(8):
            at = slice(e * 128, e * 128 + 128)
            rest_grads[e, 0:48, 1024:1152] = jnp.concatenate(
                [router_grad[:, at], gain_rows[:, at]], axis=0
            ).astype(BF)

    pair = [scatter_yz(place, mail, late, pair_sum, h, *yz) for h in (0, 1)]
    swap = swap_heads(place, mail, heads, arrived)
    pump([swap])
    output_grads[...] = weight_grads(attended, branch[...])
    output = scatter_x(place, mail, output_grads, output_mine, *output_x, 128)
    moved = scatter_x(place, mail, outs, layer_out, *x_outs, TOK, extra=after_attn)
    pump([output, moved])
    pump([output, moved])
    pump([output, moved])
    drain(swap)
    load_late.wait()
    pump(pair)
    pump([output, moved])
    unpack()
    norms_back()
    query_grads[...] = weight_grads(normed_low, grad_proj[:, 0:1024])
    query = scatter_x(place, mail, query_grads, query_mine, *query_x, 128)
    pump([query])
    pump([query])
    pump([query])
    rest_grads[:, :, 0:1024] = weight_grads(normed_low, grad_proj[:, 1024:2048])
    input_back()
    small_grads()
    others = scatter_x(place, mail, rest_grads, rest_mine, *rest_x, 128)
    pump([others])
    drain(output)
    output = sum_ctx(place, mail, output_mine, output_sum, output_slots)
    pump([output])
    pump([others])
    pump([query, others])
    pump(pair)
    drain(moved)
    drain(query)
    query = sum_ctx(place, mail, query_mine, query_sum, query_slots)
    pump([query])
    pump([output, others])
    pump(pair)
    drain(others)
    others = sum_ctx(place, mail, rest_mine, rest_sum, rest_slots)
    pump([others, query])
    drain(output)
    pump(pair)
    pump([others])
    drain(query)
    for routine in pair:
        drain(routine)
    drain(others)
    mail.finish()


REST = 1280


def dense_scratch(columns):
    return [
        pltpu.VMEM((128, columns), BF),
        pltpu.VMEM((16, SUM_ROWS, columns // 2), BF),
        pltpu.VMEM((8, 128, columns), BF),
    ]


def last_sum(*args):
    return sends(
        last_body,
        SCATTER_YZ_COPIES + 4 * SCATTER_X_COPIES + 15 + 90,
        [
            jax.ShapeDtypeStruct((2, 96, 1024), F32),
            jax.ShapeDtypeStruct((128, 1024), BF),
            jax.ShapeDtypeStruct((128, REST), BF),
            jax.ShapeDtypeStruct((128, 1024), BF),
            jax.ShapeDtypeStruct((TOK, D), F32),
            jax.ShapeDtypeStruct((TOK, D), F32),
        ],
        args,
        [vmem_spec()] * 14 + [any_spec()] * 2,
        [vmem_spec()] * 6,
        scatter_yz_scratch()
        + scatter_x_scratch(TOK, D)
        + scatter_x_scratch(128, 1024)
        + scatter_x_scratch(128, REST)
        + scatter_x_scratch(128, 1024)
        + dense_scratch(1024)
        + dense_scratch(REST)
        + dense_scratch(1024)
        + [
            pltpu.VMEM((2, 16, 96, 1024), BF),
            pltpu.VMEM((D, 2048), BF),
            pltpu.SemaphoreType.DMA((2,)),
            pltpu.VMEM((16, 3, HALF, 128), BF),
            pltpu.VMEM((TOK, 1536), F32),
            pltpu.VMEM((TOK, 2048), BF),
            pltpu.VMEM((16, 1024), F32),
        ],
        4,
    )


def smem_spec():
    return pl.BlockSpec(memory_space=pltpu.SMEM)


def spread_blocks(order, pairs):
    for c in range(16):
        spot = order[c]
        low_at = pl.ds(pl.multiple_of(spot * HALF, 16), HALF)
        high_at = pl.ds(pl.multiple_of((31 - spot) * HALF, 16), HALF)
        for src, which, dst, scale in pairs:
            block = src[c, which]
            if scale is not None:
                block = block * scale
            dst[low_at, :] = block[:, 0:HEAD]
            dst[high_at, :] = block[:, HEAD : 2 * HEAD]


def close_blocks(order, src, dst, which):
    for c in range(16):
        spot = order[c]
        low = src[pl.ds(pl.multiple_of(spot * HALF, 16), HALF), :]
        high = src[pl.ds(pl.multiple_of((31 - spot) * HALF, 16), HALF), :]
        dst[c, which] = jnp.concatenate([low, high], axis=1).astype(dst.dtype)


def doc_start(bounds, at):
    start = 0
    for d in range(3):
        start = jnp.where(at >= bounds[d], bounds[d], start)
    return start


def tile_mask(bounds, i, j, rows, keys):
    query_at = lax.broadcasted_iota(jnp.int32, (1, rows), 1) + i * rows
    key_at = lax.broadcasted_iota(jnp.int32, (keys, rows), 0) + j * keys
    start = jnp.zeros((1, rows), jnp.int32)
    for d in range(3):
        start = jnp.where(query_at >= bounds[d], bounds[d], start)
    return (key_at >= start) & (key_at <= query_at)


def key_loop(bounds, i, rows, keys, step, state):
    first = doc_start(bounds, i * rows) // keys
    clear = (doc_start(bounds, i * rows + rows - 1) + keys - 1) // keys
    edge = (i * rows) // keys
    clear = jnp.minimum(jnp.maximum(clear, first), edge)
    state = lax.fori_loop(first, clear, lambda j, s: step(j, s, True), state)
    state = lax.fori_loop(clear, edge, lambda j, s: step(j, s, False), state)
    for n in range(max(1, rows // keys)):
        state = step(edge + n, state, True)
    return state


def attend_back_body(rows, keys, order, bounds, qkv, grad_in, kept, grads, qs, ks, vs, gs, kt, dq, dk, dv):
    spread_blocks(order, [(qkv, 0, qs, 0.125), (qkv, 1, ks, None), (qkv, 2, vs, None), (grad_in, 0, gs, None)])
    dk[...] = jnp.zeros_like(dk)
    dv[...] = jnp.zeros_like(dv)
    for i in range(SEQ // 256):
        kt[:, i * 256 : i * 256 + 256] = ks[i * 256 : i * 256 + 256, :].astype(F32).T.astype(BF)
    def query_tile(i, _):
        at = pl.ds(pl.multiple_of(i * rows, rows), rows)
        query = qs[at, :]
        grad = gs[at, :]
        lse = kept[HEAD : HEAD + 1, at]
        delta = jnp.sum(kept[0:HEAD, at] * grad.astype(F32).T, axis=0, keepdims=True)
        def step(j, acc, masked):
            here = pl.ds(pl.multiple_of(j * keys, keys), keys)
            scores = dot_tt(ks[here, :], query, ((1,), (1,)))
            grad_probs = dot_tt(vs[here, :], grad, ((1,), (1,)))
            if masked:
                scores = jnp.where(tile_mask(bounds, i, j, rows, keys), scores, MASKED)
            probs = jnp.exp(scores - lse)
            grad_scores = (probs * (grad_probs - delta)).astype(BF)
            dv[here, :] += jnp.dot(probs.astype(BF), grad, preferred_element_type=F32)
            dk[here, :] += jnp.dot(grad_scores, query, preferred_element_type=F32)
            return acc + dot_tt(kt[:, here], grad_scores, ((1,), (0,)))
        acc = key_loop(bounds, i, rows, keys, step, jnp.zeros((HEAD, rows), F32))
        dq[at, :] = acc.T * 0.125
        return 0
    lax.fori_loop(0, SEQ // rows, query_tile, 0)
    close_blocks(order, dq, grads, 0)
    close_blocks(order, dk, grads, 1)
    close_blocks(order, dv, grads, 2)


def attend_back(order, bounds, qkv, grad_in, kept, rows=512, keys=256):
    return pl.pallas_call(
        functools.partial(attend_back_body, rows, keys),
        out_shape=jax.ShapeDtypeStruct((16, 3, HALF, 2 * HEAD), BF),
        in_specs=[smem_spec()] * 2 + [vmem_spec()] * 3, out_specs=vmem_spec(),
        scratch_shapes=[pltpu.VMEM((SEQ, HEAD), BF)] * 4 + [pltpu.VMEM((HEAD, SEQ), BF)] + [pltpu.VMEM((SEQ, HEAD), F32)] * 3,
        compiler_params=pltpu.CompilerParams(vmem_limit_bytes=VMEM_BYTES))(order, bounds, qkv, grad_in, kept)


def body(
    hidden_in, cotangent, segments, routes, priority, pair_order, attn_gain, w_query, w_key, w_value,
    query_gain, key_gain, w_output, ffn_gain, w_router, w_gate, w_up, w_down,
):
    misc = jnp.concatenate(
        [
            w_router.T,
            jnp.stack(
                [attn_gain, query_gain, jnp.concatenate([key_gain, jnp.zeros((64,), BF)]), ffn_gain]
            ),
            jnp.zeros((128 - 36, 128), BF),
        ]
    )
    misc = jnp.concatenate([misc, jnp.zeros((128, FRONT - 2176), BF)], axis=1)
    seg = segments[0]
    bounds = jnp.sum((seg[None, :] < jnp.arange(1, 4)[:, None]).astype(jnp.int32), axis=1)

    freqs = 10000.0 ** (-2.0 * jnp.arange(HEAD // 2, dtype=F32) / HEAD)
    freqs = jnp.concatenate([freqs] * 4)[None]
    hidden, cot = hidden_in[0], cotangent[0]
    spots = jnp.arange(16, dtype=jnp.int32)
    inverse = jnp.sum(jnp.where(pair_order[None, :] == spots[:, None], spots[None, :], 0), axis=1)
    (
        dense, w_output_all, cots, w_in, w_out, tokens,
        qkv, kept, proj, normed_low, gains, router, cosine, sine, attended, after_attn, mid_low, soft,
    ) = front(
        pair_order, inverse, bounds,
        w_query, w_key, w_value, w_output, misc, cot, routes[0], priority[0],
        priority[0].reshape(TOK, 1), w_gate, w_up, w_down, hidden, freqs,
    )
    grad_after, branch, ffn_grad, router_grad, grad_heads, early_sum, outs, late_grads = core(
        after_attn, mid_low, soft, cot, gains, router, w_output_all, tokens, cots, w_in, w_out
    )
    grad_qkv = attend_back(pair_order, bounds, qkv, grad_heads, kept)
    late_sum, query_sum, rest_sum, output_sum, grad_input, layer_out = last_sum(
        grad_qkv, proj, normed_low, attended, branch, grad_after, hidden, cosine, sine, gains,
        ffn_grad, router_grad, after_attn, outs, dense, late_grads,
    )
    rest_sum = rest_sum.astype(F32)
    expert_sum = jnp.concatenate([early_sum, late_sum])
    return (
        layer_out[None],
        grad_input[None],
        rest_sum[32, 1024:1152],
        query_sum.astype(F32),
        rest_sum[:, 0:512],
        rest_sum[:, 512:1024],
        rest_sum[33, 1024:1152],
        rest_sum[34, 1024:1088],
        output_sum.astype(F32),
        rest_sum[35, 1024:1152],
        rest_sum[0:32, 1024:1152].T,
        expert_sum[:, 0:64, 0:FF],
        expert_sum[:, 0:64, FF:],
        expert_sum[:, 64:96, :],
    )


def solution(mesh):
    exp, tok = P("exp"), P("exp", "ctx", None)
    rows = P("exp", None)
    return jax.shard_map(
        body,
        mesh=mesh,
        in_specs=(
            tok, tok, rows, tok, tok, P(), exp, rows, rows, rows, exp, exp, rows, exp, rows,
            tok, tok, tok,
        ),
        out_specs=(
            tok, tok, exp, rows, rows, rows, exp, exp, rows, exp, rows, tok, tok, tok,
        ),
        check_vma=False,
    )
```
